128 devices in a mesh: dp: 8 (over x, core), vocab: 4 (over z), width: 4 (over y).
Axes of the slice: x: 4, y: 4, z: 4, core: 2. Of those that a mesh axis runs over, the one named last changes fastest.
Arguments:
- tokens: bfloat16 [32768, 8192], P(('dp', 'vocab'), 'width'), may hold values from -300 to 300
- table: float32 [12288, 8192], P(('dp', 'vocab'), 'width'), may hold values from -6 to 6
- moment_one: float32 [12288, 8192], P(('dp', 'vocab'), 'width'), may hold values from -4 to 4
- moment_two: float32 [12288, 8192], P(('dp', 'vocab'), 'width'), may hold values from 0.01 to 1
- block_ids: int32 [8], replicated, may hold values from 0 to 95, as said below
- targets: int32 [32768], P(('dp', 'vocab')), may hold values from 0 to 1023
Outputs:
- new_table: float32 [12288, 8192], P(('dp', 'vocab'), 'width')
- new_moment_one: float32 [12288, 8192], P(('dp', 'vocab'), 'width')
- new_moment_two: float32 [12288, 8192], P(('dp', 'vocab'), 'width')
- token_grads: bfloat16 [32768, 8192], P(('dp', 'vocab'), 'width')
The draws below stay inside these ranges and needn't reach their ends.
Inputs may be any that keep to these rules, and one draw needn't show every extreme that they name: `block_ids`: the shortlist's blocks are distinct; no owner (rows of table of one device along dp+vocab, 3 blocks) holds more than 3 of them, and one owner holds exactly 3.
All inputs are finite; a program needn't handle non-finite values.
Results may differ from the reference program's by a relative error of at most 0.009.
The reference program's roundings to bfloat16 on the way (of `short_rows` and `dlogits`) count: a program that leaves them out, or rounds other values in their place, can miss the bound.
Values may be sent and summed in bfloat16 or wider, within the bound.
A program may use at most 192 MiB of HBM per device.

```python
import math
import jax
import jax.numpy as jnp
from jax import lax

D = 8192
BLOCK = 128
TOK_DEV = 1024
OWN_BLOCKS = 3
NBLK = 8
MOST = 3
SHORT = 1024
VOCAB = 12288
TOKENS = 32768
N_DP = 8
N_VOCAB = 4


def draw_tokens(key, part):
    key = jax.random.fold_in(key, 11)
    first_key = jax.random.fold_in(key, 0)
    return jnp.clip(jax.random.normal(first_key, (TOKENS, D), jnp.float32), -6.0, 6.0).astype(jnp.bfloat16)


def draw_block_ids(key, part):
    key = jax.random.fold_in(key, 23)
    first_key, second_key, third_key = jax.random.split(key, 3)
    owner_count = N_DP * N_VOCAB
    others = owner_count - 1
    busiest = jax.random.randint(first_key, (), 0, owner_count)
    slots = jnp.arange(NBLK, dtype=jnp.int32)
    rest = jnp.maximum(slots - MOST, 0)
    turn = rest % others
    index_other = jnp.where(turn % 2 == 0, others - 1 - turn // 2, turn // 2)
    other_owner = index_other + (index_other >= busiest).astype(jnp.int32)
    owner = jnp.where(slots < MOST, busiest, other_owner)
    rank = jnp.where(slots < MOST, slots, rest // others)
    owner_keys = jax.random.split(second_key, owner_count)

    def owner_perm(single_key):
        return jax.random.permutation(single_key, OWN_BLOCKS)
    perms = jax.vmap(owner_perm)(owner_keys)
    local = perms[owner, rank]
    local = jnp.where(owner == owner_count - 1, OWN_BLOCKS - 1 - rank, local)
    local = jnp.where(owner == 0, rank, local)
    ids_drawn = owner * OWN_BLOCKS + local
    order = jax.random.permutation(third_key, NBLK)
    return ids_drawn[order].astype(jnp.int32)


def place_ends(drawn, own_key, least, largest):
    spot = [jax.random.randint(jax.random.fold_in(own_key, axis), (), 0, length) for axis, length in enumerate(drawn.shape)]
    main_axis = drawn.shape.index(max(drawn.shape))
    neighbour = spot[:main_axis] + [(spot[main_axis] + 1) % drawn.shape[main_axis]] + spot[main_axis + 1:]
    return drawn.at[tuple(spot)].set(least).at[tuple(neighbour)].set(largest)


def block_scale(rng, dims, pieces, low, top_value):
    level = 1.0
    for dim, blocks in pieces:
        steps = jax.random.uniform(jax.random.fold_in(jax.random.fold_in(rng, 6), dim), (blocks,), jnp.float32, low / len(pieces), top_value / len(pieces))
        level = level * jnp.repeat(jnp.exp(steps), dims[dim] // blocks).reshape((-1,) + (1,) * (len(dims) - 1 - dim))
    return level


def gaussian(stream_key, dims, deviation, most, pieces=(), kind=jnp.bfloat16):
    loudness = block_scale(stream_key, dims, pieces, -0.22, 0.18) if pieces else 1.0
    values = jax.random.normal(stream_key, dims, jnp.float32) * deviation * loudness
    return jnp.minimum(jnp.maximum(values, -most), most).astype(kind)


def setup_inputs(seed: int = 0) -> dict:
    arg_keys = jax.random.split(jax.random.key(seed), 7)
    return {
        "tokens": draw_tokens(jax.random.fold_in(arg_keys[6], 71), 0),
        "table": gaussian(arg_keys[1], (VOCAB, D), 1.0, 6.0, ((0, 32), (1, 4)), jnp.float32),
        "moment_one": gaussian(arg_keys[2], (VOCAB, D), 0.3, 4.0, ((0, 32), (1, 4)), jnp.float32),
        "moment_two": jnp.clip(jnp.exp(math.log(1.0) - 4.6051702 * jax.random.uniform(arg_keys[3], (VOCAB, D), jnp.float32) ** block_scale(arg_keys[3], (VOCAB, D), ((0, 32), (1, 4)), -0.2, 0.2)), 0.01, 1.0),
        "block_ids": draw_block_ids(jax.random.fold_in(arg_keys[6], 71), 0),
        "targets": place_ends(jax.random.randint(arg_keys[5], (TOKENS,), 0, SHORT), jax.random.fold_in(arg_keys[5], 1), 0, SHORT - 1).astype(jnp.int32),
    }


beta_one = 0.9
beta_two = 0.95
learn_rate = 0.01
decay_rate = 0.1
epsilon = 1e-08

def adamw_rows(weights, first, second, grads):
    first_new = beta_one * first + (1.0 - beta_one) * grads
    second_new = beta_two * second + (1.0 - beta_two) * grads * grads
    correct_one = 1.0 - beta_one ** 10
    correct_two = 1.0 - beta_two ** 10
    update = first_new / correct_one / (jnp.sqrt(second_new / correct_two) + epsilon) + decay_rate * weights
    return (weights - learn_rate * update, first_new, second_new)

def reference(tokens, table, moment_one, moment_two, block_ids, targets):
    offsets = jnp.arange(BLOCK, dtype=jnp.int32)
    row_index = (block_ids[:, None] * BLOCK + offsets[None, :]).reshape(-1).astype(jnp.int32)
    short_rows = table[row_index].astype(jnp.bfloat16)
    logit_scale = 1.0 / math.sqrt(D)
    groups = TOKENS // TOK_DEV
    tok_groups = tokens.reshape(groups, TOK_DEV, D)
    tgt_groups = targets.reshape(groups, TOK_DEV)
    columns = jnp.arange(SHORT, dtype=jnp.int32)

    def one_group(carry, inputs):
        tok_block, tgt_block = inputs
        logits = lax.dot_general(tok_block, short_rows, (((1,), (1,)), ((), ())), preferred_element_type=jnp.float32) * logit_scale
        probability = jax.nn.softmax(logits, axis=1)
        onehot = (tgt_block[:, None] == columns[None, :]).astype(jnp.float32)
        dlogits = (probability - onehot).astype(jnp.bfloat16)
        grad_tok = (jnp.dot(dlogits, short_rows, preferred_element_type=jnp.float32) * logit_scale).astype(jnp.bfloat16)
        partial_grad = (lax.dot_general(dlogits, tok_block, (((0,), (0,)), ((), ())), preferred_element_type=jnp.float32) * logit_scale).astype(jnp.bfloat16)
        return (carry + partial_grad.astype(jnp.float32), grad_tok)
    start = jnp.zeros((SHORT, D), jnp.float32)
    row_grad, grad_parts = lax.scan(one_group, start, (tok_groups, tgt_groups))
    new_w, new_m, new_v = adamw_rows(table[row_index], moment_one[row_index], moment_two[row_index], row_grad)
    new_table = table.at[row_index].set(new_w)
    new_moment_one = moment_one.at[row_index].set(new_m)
    new_moment_two = moment_two.at[row_index].set(new_v)
    return (new_table, new_moment_one, new_moment_two, grad_parts.reshape(TOKENS, D))
```

```python
import functools
import math

import jax
import jax.numpy as jnp
from jax import lax
from jax.experimental import pallas as pl
from jax.experimental.pallas import tpu as pltpu
from jax.sharding import PartitionSpec as P

D = 8192
BLOCK = 128
SCALE = 1.0 / math.sqrt(D)
MESH = pl.DeviceIdType.MESH
BF16 = jnp.bfloat16
F32 = jnp.float32

beta_one = 0.9
beta_two = 0.95
learn_rate = 0.01
decay_rate = 0.1
epsilon = 1e-08

N_SEM = 111


def adamw_rows(weights, first, second, grads):
    first_new = beta_one * first + (1.0 - beta_one) * grads
    second_new = beta_two * second + (1.0 - beta_two) * grads * grads
    correct_one = 1.0 - beta_one**10
    correct_two = 1.0 - beta_two**10
    update = (
        first_new / correct_one / (jnp.sqrt(second_new / correct_two) + epsilon)
        + decay_rate * weights
    )
    return (weights - learn_rate * update, first_new, second_new)


def mod4(v):
    return lax.rem(v + 4, 4)


def rows_at(start, size):
    return pl.ds(pl.multiple_of(start, size), size)


def comm_kernel(
    ids, tokens, table, targets,
    rows_out, dl_out, grad_out,
    tok, tab, tab6, tab_send, rows, part, dl, dl_t, acc, g_send, g_recv, grad,
    sums, half_sums, rs1, rs2, rt1, rt2, y1, y2,
    send_sem, recv_sem, local_sem,
):
    dp = lax.axis_index("dp")
    z = lax.axis_index("vocab")
    y = lax.axis_index("width")
    x = dp // 2
    c = lax.rem(dp, 2)
    rank = {"x": x, "z": z, "y": y}
    pending = []

    def near(axis, step):
        if axis == "x":
            return (mod4(x + step) * 2 + c, z, y)
        if axis == "z":
            return (dp, mod4(z + step), y)
        return (dp, z, mod4(y + step))

    peer = (x * 2 + (1 - c), z, y)

    def send(src, dst, device):
        i = len(pending)
        copy = pltpu.make_async_remote_copy(
            src_ref=src, dst_ref=dst, send_sem=send_sem.at[i], recv_sem=recv_sem.at[i],
            device_id=device, device_id_type=MESH,
        )
        copy.start()
        pending.append(copy)
        return copy

    def load(src, dst, i):
        copy = pltpu.make_async_copy(src, dst, local_sem.at[i])
        copy.start()
        return copy

    tab_copy = load(table, tab, 0)
    tok_copy = load(tokens, tok, 1)

    barrier = pltpu.get_barrier_semaphore()
    partners = [near(a, s) for a in "xzy" for s in (1, -1)] + [peer]
    for device in partners:
        pl.semaphore_signal(barrier, inc=1, device_id=device, device_id_type=MESH)
    pl.semaphore_wait(barrier, len(partners))

    class Scatter:
        def __init__(self, axis, piece, first, second):
            self.axis, self.piece, self.first, self.second = axis, piece, first, second
            self.r = rank[axis]

        def far(self):
            far = mod4(self.r + 2)
            self.far_up = send(self.piece(far, 0), self.first.at[0], near(self.axis, 1))
            self.far_down = send(self.piece(far, 1), self.first.at[1], near(self.axis, -1))

        def direct(self):
            up, down = mod4(self.r + 1), mod4(self.r - 1)
            self.direct_up = send(self.piece(up, 1), self.second.at[0, 1], near(self.axis, 1))
            self.direct_down = send(self.piece(down, 0), self.second.at[1, 0], near(self.axis, -1))

        def relay(self):
            up, down = mod4(self.r + 1), mod4(self.r - 1)
            self.far_up.wait_recv()
            ref = self.piece(up, 0)
            ref[...] = (ref[...].astype(F32) + self.first[0].astype(F32)).astype(ref.dtype)
            self.relay_up = send(ref, self.second.at[0, 0], near(self.axis, 1))
            self.far_down.wait_recv()
            ref = self.piece(down, 1)
            ref[...] = (ref[...].astype(F32) + self.first[1].astype(F32)).astype(ref.dtype)
            self.relay_down = send(ref, self.second.at[1, 1], near(self.axis, -1))

        def finish(self, h):
            if h == 0:
                self.relay_up.wait_recv()
                self.direct_down.wait_recv()
            else:
                self.direct_up.wait_recv()
                self.relay_down.wait_recv()
            return (
                self.piece(self.r, h)[...].astype(F32)
                + self.second[0, h].astype(F32)
                + self.second[1, h].astype(F32)
            )

    class Gather:
        def __init__(self, axis, place):
            self.axis, self.place = axis, place
            self.r = rank[axis]

        def start(self):
            own = self.place(self.r, None)
            self.up = send(own, own, near(self.axis, 1))
            self.down = send(own, own, near(self.axis, -1))

        def relay(self):
            self.up.wait_recv()
            ref = self.place(mod4(self.r - 1), 0)
            self.relay_up = send(ref, ref, near(self.axis, 1))
            self.down.wait_recv()
            ref = self.place(mod4(self.r + 1), 1)
            self.relay_down = send(ref, ref, near(self.axis, -1))

        def finish(self):
            self.relay_up.wait_recv()
            self.relay_down.wait_recv()

    def plane_all_reduce(n, result):
        axes = (("x", "z"), ("z", "x"))
        outer = []
        for half, (a, b) in enumerate(axes):
            def piece(p, h, half=half):
                return sums.at[n, p, rows_at(half * 512 + h * 256, 256), :]
            outer.append(Scatter(a, piece, rs1.at[n, half], rs2.at[n, half]))
        for s in outer:
            s.far()
        for s in outer:
            s.direct()
        for s in outer:
            s.relay()
        inner = []
        for half, (a, b) in enumerate(axes):
            for h in range(2):
                half_sums[n, half, h * 256:(h + 1) * 256, :] = outer[half].finish(h).astype(BF16)
            def piece(p, h, half=half):
                return half_sums.at[n, half, rows_at(p * 128 + h * 64, 64), :]
            s = Scatter(b, piece, rt1.at[n, half], rt2.at[n, half])
            s.far()
            s.direct()
            inner.append(s)
        for s in inner:
            s.relay()
        gathers = []
        for half, (a, b) in enumerate(axes):
            chunk = c * 4 + rank[a]
            for h in range(2):
                result[chunk, rows_at(half * 512 + rank[b] * 128 + h * 64, 64), :] = (
                    inner[half].finish(h).astype(BF16)
                )
            def place(p, h, half=half, chunk=chunk):
                if h is None:
                    return result.at[chunk, rows_at(half * 512 + p * 128, 128), :]
                return result.at[chunk, rows_at(half * 512 + p * 128 + h * 64, 64), :]
            s = Gather(b, place)
            s.start()
            gathers.append(s)
        for s in gathers:
            s.relay()
        outer = []
        across = []

        def hand_over(p, half):
            ref = result.at[c * 4 + p, rows_at(half * 512, 512), :]
            across.append(send(ref, ref, peer))

        for half, (a, b) in enumerate(axes):
            gathers[half].finish()
            def place(p, h, half=half):
                if h is None:
                    return result.at[c * 4 + p, rows_at(half * 512, 512), :]
                return result.at[c * 4 + p, rows_at(half * 512 + h * 256, 256), :]
            s = Gather(a, place)
            s.start()
            outer.append(s)
            hand_over(rank[a], half)
        for half, s in enumerate(outer):
            s.relay()
            hand_over(mod4(s.r - 1), half)
            hand_over(mod4(s.r + 1), half)
        for half, s in enumerate(outer):
            s.finish()
            hand_over(mod4(s.r + 2), half)
        for copy in across:
            copy.wait_recv()

    tab_copy.wait()
    for k in range(4):
        cols = pl.ds(pl.multiple_of((1 - c) * 1024 + k * 256, 256), 256)
        for j in range(3):
            tab_send[j, k] = tab[j * BLOCK:(j + 1) * BLOCK, cols].astype(BF16)
    table_half = send(tab_send, tab6.at[pl.ds(c * 3, 3)], peer)
    for k in range(4):
        cols = pl.ds(pl.multiple_of(c * 1024 + k * 256, 256), 256)
        for j in range(3):
            tab6[c * 3 + j, k] = tab[j * BLOCK:(j + 1) * BLOCK, cols].astype(BF16)
    table_half.wait_recv()
    for b in range(8):
        block = ids[b]
        owner = block // 3
        owner_dp = owner // 4
        here = jnp.logical_and(lax.rem(owner, 4) == z, owner_dp // 2 == x)
        slot = lax.rem(owner_dp, 2) * 3 + lax.rem(block, 3)
        for k in range(4):
            sums[0, k, b * BLOCK:(b + 1) * BLOCK, :] = jnp.where(
                here, tab6[slot, k].astype(F32), 0.0
            ).astype(BF16)
    plane_all_reduce(0, rows)
    rows_copy = load(rows, rows_out, 2)

    tok_copy.wait()

    def logits_of(p):
        @pl.loop(0, 4)
        def _(n):
            total = jnp.zeros((256, 256), F32)
            for k in range(8):
                total += lax.dot_general(
                    tok[rows_at(p * 256, 256), k * 256:(k + 1) * 256],
                    rows[k, rows_at(n * 256, 256), :],
                    (((1,), (1,)), ((), ())),
                    preferred_element_type=F32,
                )
            part[rows_at(p * 256, 256), pl.ds(pl.multiple_of(n * 256, 256), 256)] = total

    def part_piece(p, h):
        return part.at[rows_at(p * 256 + h * 128, 128), :]

    s = Scatter("y", part_piece, y1, y2)
    logits_of(mod4(y + 2))
    s.far()
    logits_of(mod4(y + 1))
    logits_of(mod4(y - 1))
    s.direct()
    logits_of(y)
    s.relay()

    for h in range(2):
        logits = s.finish(h) * SCALE
        exponent = jnp.exp(logits - jnp.max(logits, axis=1, keepdims=True))
        probability = exponent * (1.0 / jnp.sum(exponent, axis=1, keepdims=True))
        line = targets[pl.ds(y * 2 + h, 1), :].astype(F32)
        column = jnp.transpose(jnp.broadcast_to(line, (128, 128)))[:, :1]
        place = lax.broadcasted_iota(jnp.int32, (128, 1024), 1).astype(F32)
        onehot = jnp.where(column == place, 1.0, 0.0)
        dl[rows_at(y * 256 + h * 128, 128), :] = (probability - onehot).astype(BF16)

    def dl_place(p, h):
        if h is None:
            return dl.at[rows_at(p * 256, 256), :]
        return dl.at[rows_at(p * 256 + h * 128, 128), :]

    g = Gather("y", dl_place)
    g.start()

    def turn(p):
        dl_t[p] = jnp.transpose(dl[rows_at(p * 256, 256), :])

    def product(p, k, n):
        return jnp.dot(
            dl_t[p, rows_at(n * 512, 512), :],
            tok[rows_at(p * 256, 256), pl.ds(pl.multiple_of(k * 256, 256), 256)],
            preferred_element_type=F32,
        )

    def each_tile(f):
        @pl.loop(0, 8)
        def _(k):
            @pl.loop(0, 2)
            def _(n):
                f(k, n)

    turn(y)

    def first(k, n):
        acc[k, rows_at(n * 512, 512), :] = product(y, k, n)

    each_tile(first)
    g.relay()
    up, down, far = mod4(y + 1), mod4(y - 1), mod4(y + 2)
    turn(up)
    turn(down)

    def second(k, n):
        acc[k, rows_at(n * 512, 512), :] += product(up, k, n) + product(down, k, n)

    each_tile(second)
    g.finish()
    dl_copy = load(dl, dl_out, 3)
    turn(far)

    crossing = []
    for q in range(4):
        k = (1 - c) * 4 + q
        @pl.loop(0, 2)
        def _(n):
            here = rows_at(n * 512, 512)
            g_send[q, here, :] = ((acc[k, here, :] + product(far, k, n)) * SCALE).astype(BF16)
        crossing.append(send(g_send.at[q], g_recv.at[q], peer))
    for q in range(4):
        k = c * 4 + q
        crossing[q].wait_recv()
        @pl.loop(0, 2)
        def _(n):
            here = rows_at(n * 512, 512)
            total = (acc[k, here, :] + product(far, k, n)) * SCALE
            sums[1, q, here, :] = (total + g_recv[q, here, :].astype(F32)).astype(BF16)
    plane_all_reduce(1, grad)
    grad_copy = load(grad, grad_out, 4)

    assert len(pending) == N_SEM, len(pending)
    for copy in pending:
        copy.wait_send()
    rows_copy.wait()
    dl_copy.wait()
    grad_copy.wait()


def communicate(ids, tokens, table, targets):
    vmem = pltpu.VMEM
    return pl.pallas_call(
        comm_kernel,
        out_shape=(
            jax.ShapeDtypeStruct((8, 1024, 256), BF16),
            jax.ShapeDtypeStruct((1024, 1024), BF16),
            jax.ShapeDtypeStruct((8, 1024, 256), BF16),
        ),
        in_specs=[
            pl.BlockSpec(memory_space=pltpu.SMEM),
            pl.BlockSpec(memory_space=pl.ANY),
            pl.BlockSpec(memory_space=pl.ANY),
            pl.BlockSpec(memory_space=pltpu.VMEM),
        ],
        out_specs=(pl.BlockSpec(memory_space=pl.ANY),) * 3,
        scratch_shapes=[
            vmem((1024, 2048), BF16),
            vmem((384, 2048), F32),
            vmem((6, 4, 128, 256), BF16),
            vmem((3, 4, 128, 256), BF16),
            vmem((8, 1024, 256), BF16),
            vmem((1024, 1024), F32),
            vmem((1024, 1024), BF16),
            vmem((4, 1024, 256), BF16),
            vmem((8, 1024, 256), F32),
            vmem((4, 1024, 256), BF16),
            vmem((4, 1024, 256), BF16),
            vmem((8, 1024, 256), BF16),
            vmem((2, 4, 1024, 256), BF16),
            vmem((2, 2, 512, 256), BF16),
            vmem((2, 2, 2, 256, 256), BF16),
            vmem((2, 2, 2, 2, 256, 256), BF16),
            vmem((2, 2, 2, 64, 256), BF16),
            vmem((2, 2, 2, 2, 64, 256), BF16),
            vmem((2, 128, 1024), F32),
            vmem((2, 2, 128, 1024), F32),
            pltpu.SemaphoreType.DMA((N_SEM,)),
            pltpu.SemaphoreType.DMA((N_SEM,)),
            pltpu.SemaphoreType.DMA((5,)),
        ],
        compiler_params=pltpu.CompilerParams(
            collective_id=0, has_side_effects=True, vmem_limit_bytes=60 * 2**20
        ),
    )(ids, tokens, table, targets)


def update_kernel(
    where_ref, dl, rows, g0, g1, g2, w, m, v, w_out, m_out, v_out, tok_out
):
    tok_out[...] = (
        jnp.dot(dl[...], rows[0], preferred_element_type=F32) * SCALE
    ).astype(BF16)
    for j, g in enumerate((g0, g1, g2)):
        here = slice(j * BLOCK, (j + 1) * BLOCK)
        listed = where_ref[3 + j] > 0
        old = (w[here, :], m[here, :], v[here, :])
        new = adamw_rows(*old, g[0].astype(F32))
        w_out[here, :] = jnp.where(listed, new[0], old[0])
        m_out[here, :] = jnp.where(listed, new[1], old[1])
        v_out[here, :] = jnp.where(listed, new[2], old[2])


def update(where, dl, rows, grad, table, moment_one, moment_two):
    wide = pl.BlockSpec((384, 256), lambda k, s: (0, k))
    grad_spec = [
        pl.BlockSpec((1, BLOCK, 256), lambda k, s, j=j: (k, s[j], 0)) for j in range(3)
    ]
    return pl.pallas_call(
        update_kernel,
        grid_spec=pltpu.PrefetchScalarGridSpec(
            num_scalar_prefetch=1,
            grid=(8,),
            in_specs=[
                pl.BlockSpec((1024, 1024), lambda k, s: (0, 0)),
                pl.BlockSpec((1, 1024, 256), lambda k, s: (k, 0, 0)),
                *grad_spec,
                wide, wide, wide,
            ],
            out_specs=[wide, wide, wide, pl.BlockSpec((1024, 256), lambda k, s: (0, k))],
        ),
        out_shape=[jax.ShapeDtypeStruct((384, 2048), F32)] * 3
        + [jax.ShapeDtypeStruct((1024, 2048), BF16)],
        compiler_params=pltpu.CompilerParams(vmem_limit_bytes=48 * 2**20),
    )(where, dl, rows, grad, grad, grad, table, moment_one, moment_two)


def body(tokens, table, moment_one, moment_two, block_ids, targets):
    owner = lax.axis_index(("dp", "vocab"))
    mine = owner * 3 + jnp.arange(3, dtype=jnp.int32)
    match = block_ids[None, :] == mine[:, None]
    listed = jnp.any(match, axis=1).astype(jnp.int32)
    place = jnp.argmax(match, axis=1).astype(jnp.int32)
    where = jnp.concatenate([place, listed])
    rows, dl, grad = communicate(block_ids, tokens, table, targets.reshape(8, 128))
    return tuple(update(where, dl, rows, grad, table, moment_one, moment_two))


def solution(mesh):
    wide = P(("dp", "vocab"), "width")
    return jax.shard_map(
        body,
        mesh=mesh,
        in_specs=(wide, wide, wide, wide, P(), P(("dp", "vocab"))),
        out_specs=(wide, wide, wide, wide),
        check_vma=False,
    )
```

```python
import functools
import math

import jax
import jax.numpy as jnp
from jax import lax
from jax.experimental import pallas as pl
from jax.experimental.pallas import tpu as pltpu
from jax.sharding import PartitionSpec as P

D = 8192
BLOCK = 128
SCALE = 1.0 / math.sqrt(D)
MESH = pl.DeviceIdType.MESH
BF16 = jnp.bfloat16
F32 = jnp.float32
WIRE = jnp.int16
STEPS = 32700.0
LOG_STEP = 256.0

beta_one = 0.9
beta_two = 0.95
learn_rate = 0.01
decay_rate = 0.1
epsilon = 1e-08

N_SEM = 289


def adamw_rows(weights, first, second, grads):
    first_new = beta_one * first + (1.0 - beta_one) * grads
    second_new = beta_two * second + (1.0 - beta_two) * grads * grads
    correct_one = 1.0 - beta_one**10
    correct_two = 1.0 - beta_two**10
    update = (
        first_new / correct_one / (jnp.sqrt(second_new / correct_two) + epsilon)
        + decay_rate * weights
    )
    return (weights - learn_rate * update, first_new, second_new)


def mod4(v):
    return lax.rem(v + 4, 4)


def rows_at(start, size):
    return pl.ds(pl.multiple_of(start, size), size)


def comm_kernel(
    ids, tokens, table, targets,
    rows_out, dl_out, grad_out,
    tok, tab, tab6, tab_send, rows, part, wire, dl, dl_t, acc, g_send, g_recv, grad,
    sums, half_sums, rs1, rs2, rt1, rt2, y1, y2, column,
    send_sem, recv_sem, local_sem,
):
    dp = lax.axis_index("dp")
    z = lax.axis_index("vocab")
    y = lax.axis_index("width")
    x = dp // 2
    c = lax.rem(dp, 2)
    rank = {"x": x, "z": z, "y": y}
    pending = []

    def near(axis, step):
        if axis == "x":
            return (mod4(x + step) * 2 + c, z, y)
        if axis == "z":
            return (dp, mod4(z + step), y)
        return (dp, z, mod4(y + step))

    peer = (x * 2 + (1 - c), z, y)

    def send(src, dst, device):
        i = len(pending)
        copy = pltpu.make_async_remote_copy(
            src_ref=src, dst_ref=dst, send_sem=send_sem.at[i], recv_sem=recv_sem.at[i],
            device_id=device, device_id_type=MESH,
        )
        copy.start()
        pending.append(copy)
        return copy

    def load(src, dst, i):
        copy = pltpu.make_async_copy(src, dst, local_sem.at[i])
        copy.start()
        return copy

    tab_copy = load(table, tab, 0)
    tok_copy = load(tokens, tok, 1)

    barrier = pltpu.get_barrier_semaphore()
    partners = [near(a, s) for a in "xzy" for s in (1, -1)] + [peer]
    for device in partners:
        pl.semaphore_signal(barrier, inc=1, device_id=device, device_id_type=MESH)
    pl.semaphore_wait(barrier, len(partners))

    class Scatter:
        def __init__(self, axis, piece, first, second):
            self.axis, self.piece, self.first, self.second = axis, piece, first, second
            self.r = rank[axis]
            self.above, self.below = mod4(self.r + 1), mod4(self.r - 1)
            self.up, self.down = near(axis, 1), near(axis, -1)

        def far(self):
            far = mod4(self.r + 2)
            self.far_up = send(self.piece(far, 0), self.first.at[0], self.up)
            self.far_down = send(self.piece(far, 1), self.first.at[1], self.down)

        def direct_up(self):
            self.own_up = send(self.piece(self.above, 1), self.second.at[0, 1], self.up)

        def direct_down(self):
            self.own_down = send(self.piece(self.below, 0), self.second.at[1, 0], self.down)

        def direct(self):
            self.direct_up()
            self.direct_down()

        def add(self, p, h, more):
            ref = self.piece(p, h)
            ref[...] = (ref[...].astype(F32) + more[...].astype(F32)).astype(ref.dtype)
            return ref

        def relay_up(self):
            self.far_up.wait_recv()
            ref = self.add(self.above, 0, self.first.at[0])
            self.sum_up = send(ref, self.second.at[0, 0], self.up)

        def relay_down(self):
            self.far_down.wait_recv()
            ref = self.add(self.below, 1, self.first.at[1])
            self.sum_down = send(ref, self.second.at[1, 1], self.down)

        def relay(self):
            self.relay_up()
            self.relay_down()

        def arrived(self):
            self.sum_up.wait_recv()
            self.own_down.wait_recv()
            self.own_up.wait_recv()
            self.sum_down.wait_recv()

        def total(self, h):
            return (
                self.piece(self.r, h)[...].astype(F32)
                + self.second[0, h].astype(F32)
                + self.second[1, h].astype(F32)
            )

    class Gather:
        def __init__(self, axis, place):
            self.axis, self.place = axis, place
            self.r = rank[axis]

        def start(self):
            own = self.place(self.r, None)
            self.up = send(own, own, near(self.axis, 1))
            self.down = send(own, own, near(self.axis, -1))

        def relay_up(self):
            self.up.wait_recv()
            ref = self.place(mod4(self.r - 1), 0)
            self.next_up = send(ref, ref, near(self.axis, 1))

        def relay_down(self):
            self.down.wait_recv()
            ref = self.place(mod4(self.r + 1), 1)
            self.next_down = send(ref, ref, near(self.axis, -1))

        def relay(self):
            self.relay_up()
            self.relay_down()

        def finish(self):
            self.next_up.wait_recv()
            self.next_down.wait_recv()

    def plane_all_reduce(n, result):
        halves = range(2)
        axes = (("x", "z"), ("z", "x"))

        def blocks_of(half):
            r = rank[axes[half][1]]
            return [mod4(r + 2), mod4(r + 1), mod4(r - 1), r]

        outer = [[], []]
        inner = []
        for half, (a, b) in enumerate(axes):
            for i, block in enumerate(blocks_of(half)):
                def piece(p, h, half=half, block=block):
                    return sums.at[n, p, rows_at(half * 512 + block * 128 + h * 64, 64), :]
                outer[half].append(Scatter(a, piece, rs1.at[n, half, i], rs2.at[n, half, i]))
            def piece(p, h, half=half):
                return half_sums.at[n, half, rows_at(p * 128 + h * 64, 64), :]
            inner.append(Scatter(b, piece, rt1.at[n, half], rt2.at[n, half]))

        def finish(half, i):
            outer[half][i].arrived()
            block = blocks_of(half)[i]
            for h in range(2):
                half_sums[n, half, rows_at(block * 128 + h * 64, 64), :] = (
                    outer[half][i].total(h).astype(BF16)
                )

        for i in range(4):
            for half in halves:
                outer[half][i].far()
            if i >= 1:
                for half in halves:
                    outer[half][i - 1].direct()
        for half in halves:
            outer[half][3].direct()
        for half in halves:
            outer[half][0].relay()
        for half in halves:
            outer[half][1].relay()
        for half in halves:
            finish(half, 0)
            inner[half].far()
        for half in halves:
            outer[half][2].relay()
        for half in halves:
            finish(half, 1)
            inner[half].direct_up()
        for half in halves:
            outer[half][3].relay()
        for half in halves:
            inner[half].relay_up()
            finish(half, 2)
            inner[half].direct_down()
            inner[half].relay_down()
        for half in halves:
            finish(half, 3)

        across = []
        inner_gather = []
        outer_gather = [[], []]

        def hand_over(half, p, block):
            ref = result.at[c * 4 + p, rows_at(half * 512 + block * 128, 128), :]
            across.append(send(ref, ref, peer))

        def spread(half, block):
            a = axes[half][0]
            def place(p, h):
                if h is None:
                    return result.at[c * 4 + p, rows_at(half * 512 + block * 128, 128), :]
                return result.at[c * 4 + p, rows_at(half * 512 + block * 128 + h * 64, 64), :]
            g = Gather(a, place)
            g.start()
            outer_gather[half].append((g, block))
            hand_over(half, rank[a], block)

        for half, (a, b) in enumerate(axes):
            chunk = c * 4 + rank[a]
            inner[half].arrived()
            for h in range(2):
                result[chunk, rows_at(half * 512 + rank[b] * 128 + h * 64, 64), :] = (
                    inner[half].total(h).astype(BF16)
                )
            def place(p, h, half=half, chunk=chunk):
                if h is None:
                    return result.at[chunk, rows_at(half * 512 + p * 128, 128), :]
                return result.at[chunk, rows_at(half * 512 + p * 128 + h * 64, 64), :]
            g = Gather(b, place)
            g.start()
            inner_gather.append(g)
            spread(half, rank[b])

        def spread_relay(half, i):
            g, block = outer_gather[half][i]
            g.relay_up()
            hand_over(half, mod4(g.r - 1), block)
            g.relay_down()
            hand_over(half, mod4(g.r + 1), block)

        def spread_finish(half, i):
            g, block = outer_gather[half][i]
            g.finish()
            hand_over(half, mod4(g.r + 2), block)

        for half in halves:
            g = inner_gather[half]
            g.relay_up()
            spread(half, mod4(g.r - 1))
            g.relay_down()
            spread(half, mod4(g.r + 1))
        for half in halves:
            spread_relay(half, 0)
        for half in halves:
            g = inner_gather[half]
            g.finish()
            spread(half, mod4(g.r + 2))
        for half in halves:
            spread_relay(half, 1)
            spread_relay(half, 2)
        for half in halves:
            spread_finish(half, 0)
        for half in halves:
            spread_relay(half, 3)
        for half in halves:
            for i in range(1, 4):
                spread_finish(half, i)
        for copy in across:
            copy.wait_recv()

    tab_copy.wait()
    for k in range(4):
        cols = pl.ds(pl.multiple_of((1 - c) * 1024 + k * 256, 256), 256)
        for j in range(3):
            tab_send[j, k] = tab[j * BLOCK:(j + 1) * BLOCK, cols].astype(BF16)
    table_half = send(tab_send, tab6.at[pl.ds(c * 3, 3)], peer)
    for k in range(4):
        cols = pl.ds(pl.multiple_of(c * 1024 + k * 256, 256), 256)
        for j in range(3):
            tab6[c * 3 + j, k] = tab[j * BLOCK:(j + 1) * BLOCK, cols].astype(BF16)
    table_half.wait_recv()
    for b in range(8):
        block = ids[b]
        owner = block // 3
        owner_dp = owner // 4
        here = jnp.logical_and(lax.rem(owner, 4) == z, owner_dp // 2 == x)
        slot = lax.rem(owner_dp, 2) * 3 + lax.rem(block, 3)
        for k in range(4):
            sums[0, k, b * BLOCK:(b + 1) * BLOCK, :] = jnp.where(
                here, tab6[slot, k].astype(F32), 0.0
            ).astype(BF16)
    plane_all_reduce(0, rows)
    rows_copy = load(rows, rows_out, 2)

    tok_copy.wait()

    def logits_of(p):
        @pl.loop(0, 4)
        def _(n):
            total = jnp.zeros((256, 256), F32)
            for k in range(8):
                total += lax.dot_general(
                    tok[rows_at(p * 256, 256), k * 256:(k + 1) * 256],
                    rows[k, rows_at(n * 256, 256), :],
                    (((1,), (1,)), ((), ())),
                    preferred_element_type=F32,
                )
            part[rows_at(p * 256, 256), pl.ds(pl.multiple_of(n * 256, 256), 256)] = total * SCALE

    def encode(start):
        @pl.loop(0, 4)
        def _(t):
            some = rows_at(start + t * 16, 16)
            value = part[some, :]
            peak = jnp.max(jnp.abs(value), axis=1, keepdims=True)
            power = jnp.ceil(jnp.log(jnp.maximum(peak, 1e-18)) * LOG_STEP)
            steps = value * (jnp.exp(power * (-1.0 / LOG_STEP)) * STEPS)
            wire[some, :1024] = jnp.round(steps).astype(jnp.int32).astype(WIRE)
            wire[some, 1024:] = jnp.broadcast_to(power, (16, 128)).astype(jnp.int32).astype(WIRE)

    def decode(message):
        power = message[:, 1024:].astype(F32)[:, :1]
        return message[:, :1024].astype(F32) * (jnp.exp(power * (1.0 / LOG_STEP)) * (1.0 / STEPS))

    class LogitScatter(Scatter):
        def __init__(self, u):
            self.u = u
            super().__init__("y", self.encoded, y1.at[u], y2.at[u])

        def start(self, p, h):
            return pl.multiple_of(p * 256 + self.u * 128 + h * 64, 64)

        def encoded(self, p, h):
            encode(self.start(p, h))
            return wire.at[rows_at(self.start(p, h), 64), :]

        def add(self, p, h, more):
            @pl.loop(0, 4)
            def _(t):
                part[rows_at(self.start(p, h) + t * 16, 16), :] += decode(more[rows_at(t * 16, 16), :])
            return self.encoded(p, h)

    parts = [LogitScatter(u) for u in range(2)]
    logits_of(mod4(y + 2))
    parts[0].far()
    parts[1].far()
    logits_of(mod4(y + 1))
    parts[0].direct_up()
    logits_of(mod4(y - 1))
    parts[0].direct_down()
    parts[0].relay()
    parts[1].direct()
    logits_of(y)
    parts[1].relay()

    gathers = []
    for u in range(2):
        parts[u].arrived()
        line = targets[pl.ds(y * 2 + u, 1), :].astype(F32)
        column[...] = jnp.transpose(jnp.broadcast_to(line, (128, 128)))

        @pl.loop(0, 4)
        def _(t):
            h, some = t // 2, rows_at(lax.rem(t, 2) * 32, 32)
            logits = (
                part[rows_at(y * 256 + u * 128 + t * 32, 32), :]
                + decode(y2[u, 0, h, some, :])
                + decode(y2[u, 1, h, some, :])
            )
            exponent = jnp.exp(logits - jnp.max(logits, axis=1, keepdims=True))
            probability = exponent * (1.0 / jnp.sum(exponent, axis=1, keepdims=True))
            place = lax.broadcasted_iota(jnp.int32, (32, 1024), 1).astype(F32)
            onehot = jnp.where(column[rows_at(t * 32, 32), :1] == place, 1.0, 0.0)
            dl[rows_at(y * 256 + u * 128 + t * 32, 32), :] = (probability - onehot).astype(BF16)

        def dl_place(p, h, u=u):
            if h is None:
                return dl.at[rows_at(p * 256 + u * 128, 128), :]
            return dl.at[rows_at(p * 256 + u * 128 + h * 64, 64), :]

        g = Gather("y", dl_place)
        g.start()
        gathers.append(g)
    gathers[0].relay()

    def turn(p):
        dl_t[p] = jnp.transpose(dl[rows_at(p * 256, 256), :])

    def product(p, k, n):
        return jnp.dot(
            dl_t[p, rows_at(n * 512, 512), :],
            tok[rows_at(p * 256, 256), pl.ds(pl.multiple_of(k * 256, 256), 256)],
            preferred_element_type=F32,
        )

    def each_tile(f):
        @pl.loop(0, 8)
        def _(k):
            @pl.loop(0, 2)
            def _(n):
                f(k, n)

    turn(y)

    def first(k, n):
        acc[k, rows_at(n * 512, 512), :] = product(y, k, n)

    each_tile(first)
    gathers[1].relay()
    up, down, far = mod4(y + 1), mod4(y - 1), mod4(y + 2)
    turn(up)
    turn(down)

    def second(k, n):
        acc[k, rows_at(n * 512, 512), :] += product(up, k, n) + product(down, k, n)

    each_tile(second)
    for g in gathers:
        g.finish()
    dl_copy = load(dl, dl_out, 3)
    turn(far)

    crossing = []
    for q in range(4):
        k = (1 - c) * 4 + q
        @pl.loop(0, 2)
        def _(n):
            here = rows_at(n * 512, 512)
            g_send[q, here, :] = ((acc[k, here, :] + product(far, k, n)) * SCALE).astype(BF16)
        crossing.append(send(g_send.at[q], g_recv.at[q], peer))
    for q in range(4):
        k = c * 4 + q
        crossing[q].wait_recv()
        @pl.loop(0, 2)
        def _(n):
            here = rows_at(n * 512, 512)
            total = (acc[k, here, :] + product(far, k, n)) * SCALE
            sums[1, q, here, :] = (total + g_recv[q, here, :].astype(F32)).astype(BF16)
    plane_all_reduce(1, grad)
    grad_copy = load(grad, grad_out, 4)

    assert len(pending) == N_SEM, len(pending)
    for copy in pending:
        copy.wait_send()
    rows_copy.wait()
    dl_copy.wait()
    grad_copy.wait()


def communicate(ids, tokens, table, targets):
    vmem = pltpu.VMEM
    return pl.pallas_call(
        comm_kernel,
        out_shape=(
            jax.ShapeDtypeStruct((8, 1024, 256), BF16),
            jax.ShapeDtypeStruct((1024, 1024), BF16),
            jax.ShapeDtypeStruct((8, 1024, 256), BF16),
        ),
        in_specs=[
            pl.BlockSpec(memory_space=pltpu.SMEM),
            pl.BlockSpec(memory_space=pl.ANY),
            pl.BlockSpec(memory_space=pl.ANY),
            pl.BlockSpec(memory_space=pltpu.VMEM),
        ],
        out_specs=(pl.BlockSpec(memory_space=pl.ANY),) * 3,
        scratch_shapes=[
            vmem((1024, 2048), BF16),
            vmem((384, 2048), F32),
            vmem((6, 4, 128, 256), BF16),
            vmem((3, 4, 128, 256), BF16),
            vmem((8, 1024, 256), BF16),
            vmem((1024, 1024), F32),
            vmem((1024, 1152), WIRE),
            vmem((1024, 1024), BF16),
            vmem((4, 1024, 256), BF16),
            vmem((8, 1024, 256), F32),
            vmem((4, 1024, 256), BF16),
            vmem((4, 1024, 256), BF16),
            vmem((8, 1024, 256), BF16),
            vmem((2, 4, 1024, 256), BF16),
            vmem((2, 2, 512, 256), BF16),
            vmem((2, 2, 4, 2, 64, 256), BF16),
            vmem((2, 2, 4, 2, 2, 64, 256), BF16),
            vmem((2, 2, 2, 64, 256), BF16),
            vmem((2, 2, 2, 2, 64, 256), BF16),
            vmem((2, 2, 64, 1152), WIRE),
            vmem((2, 2, 2, 64, 1152), WIRE),
            vmem((128, 128), F32),
            pltpu.SemaphoreType.DMA((N_SEM,)),
            pltpu.SemaphoreType.DMA((N_SEM,)),
            pltpu.SemaphoreType.DMA((5,)),
        ],
        compiler_params=pltpu.CompilerParams(
            collective_id=0, has_side_effects=True, vmem_limit_bytes=60 * 2**20
        ),
    )(ids, tokens, table, targets)


def listed_at(where, j):
    place, listed = 0, 0
    for b in range(8):
        same = where[b] == where[8] + j
        place = jnp.where(same, b, place)
        listed = jnp.where(same, 1, listed)
    return place, listed


def update_kernel(
    where_ref, dl, rows, g0, g1, g2, w, m, v, w_out, m_out, v_out, tok_out
):
    tok_out[...] = (
        jnp.dot(dl[...], rows[0], preferred_element_type=F32) * SCALE
    ).astype(BF16)
    for j, g in enumerate((g0, g1, g2)):
        here = slice(j * BLOCK, (j + 1) * BLOCK)
        listed = listed_at(where_ref, j)[1] > 0
        old = (w[here, :], m[here, :], v[here, :])
        new = adamw_rows(*old, g[0].astype(F32))
        w_out[here, :] = jnp.where(listed, new[0], old[0])
        m_out[here, :] = jnp.where(listed, new[1], old[1])
        v_out[here, :] = jnp.where(listed, new[2], old[2])


def update(where, dl, rows, grad, table, moment_one, moment_two):
    wide = pl.BlockSpec((384, 256), lambda k, s: (0, k))
    grad_spec = [
        pl.BlockSpec((1, BLOCK, 256), lambda k, s, j=j: (k, listed_at(s, j)[0], 0)) for j in range(3)
    ]
    return pl.pallas_call(
        update_kernel,
        grid_spec=pltpu.PrefetchScalarGridSpec(
            num_scalar_prefetch=1,
            grid=(8,),
            in_specs=[
                pl.BlockSpec((1024, 1024), lambda k, s: (0, 0)),
                pl.BlockSpec((1, 1024, 256), lambda k, s: (k, 0, 0)),
                *grad_spec,
                wide, wide, wide,
            ],
            out_specs=[wide, wide, wide, pl.BlockSpec((1024, 256), lambda k, s: (0, k))],
        ),
        out_shape=[jax.ShapeDtypeStruct((384, 2048), F32)] * 3
        + [jax.ShapeDtypeStruct((1024, 2048), BF16)],
        compiler_params=pltpu.CompilerParams(vmem_limit_bytes=48 * 2**20),
    )(where, dl, rows, grad, grad, grad, table, moment_one, moment_two)


def body(tokens, table, moment_one, moment_two, block_ids, targets):
    owner = lax.axis_index(("dp", "vocab"))
    where = jnp.concatenate([block_ids, jnp.reshape(owner * 3, (1,)).astype(jnp.int32)])
    rows, dl, grad = communicate(block_ids, tokens, table, targets.reshape(8, 128))
    return tuple(update(where, dl, rows, grad, table, moment_one, moment_two))


def solution(mesh):
    wide = P(("dp", "vocab"), "width")
    return jax.shard_map(
        body,
        mesh=mesh,
        in_specs=(wide, wide, wide, wide, P(), P(("dp", "vocab"))),
        out_specs=(wide, wide, wide, wide),
        check_vma=False,
    )
```

```python
import functools
import math

import jax
import jax.numpy as jnp
from jax import lax
from jax.experimental import pallas as pl
from jax.experimental.pallas import tpu as pltpu
from jax.sharding import PartitionSpec as P

D = 8192
BLOCK = 128
SCALE = 1.0 / math.sqrt(D)
MESH = pl.DeviceIdType.MESH
BF16 = jnp.bfloat16
F32 = jnp.float32
WIRE = jnp.int16
STEPS = 32700.0
LOG_STEP = 256.0

beta_one = 0.9
beta_two = 0.95
learn_rate = 0.01
decay_rate = 0.1
epsilon = 1e-08

RELAYED = 2
N_SEND = 25
N_RECV = 181


def adamw_rows(weights, first, second, grads):
    first_new = beta_one * first + (1.0 - beta_one) * grads
    second_new = beta_two * second + (1.0 - beta_two) * grads * grads
    correct_one = 1.0 - beta_one**10
    correct_two = 1.0 - beta_two**10
    squared = second_new * (1.0 / correct_two)
    update = (
        first_new * (1.0 / correct_one) / (squared * lax.rsqrt(squared) + epsilon)
        + decay_rate * weights
    )
    return (weights - learn_rate * update, first_new, second_new)


def mod4(v):
    return lax.rem(v + 4, 4)


def rows_at(start, size):
    return pl.ds(pl.multiple_of(start, size), size)


def comm_kernel(
    ids, tokens, table, targets,
    tok_out, grad_out,
    tok, target, tab6, tab_send, rows, part, wire, dl, dl_t, acc, g_recv, grad, picked,
    sums, half_sums, rs1, rs2, rs3, land, y1, y2, column,
    send_sem, recv_sem, plane_send, local_sem, across_send, across_recv,
):
    dp = lax.axis_index("dp")
    z = lax.axis_index("vocab")
    y = lax.axis_index("width")
    x = dp // 2
    c = lax.rem(dp, 2)
    rank = {"x": x, "z": z, "y": y}
    pending = []

    def near(axis, step):
        if axis == "x":
            return (mod4(x + step) * 2 + c, z, y)
        if axis == "z":
            return (dp, mod4(z + step), y)
        return (dp, z, mod4(y + step))

    peer = (x * 2 + (1 - c), z, y)

    landed = []
    phase = []

    def send(src, dst, device):
        left = plane_send.at[phase[0]] if phase else send_sem.at[len(pending)]
        copy = pltpu.make_async_remote_copy(
            src_ref=src, dst_ref=dst, send_sem=left, recv_sem=recv_sem.at[len(landed)],
            device_id=device, device_id_type=MESH,
        )
        copy.start()
        landed.append(copy)
        if not phase:
            pending.append(copy)
        return copy

    def load(src, dst, i):
        copy = pltpu.make_async_copy(src, dst, local_sem.at[i])
        copy.start()
        return copy

    tab_copies = [
        load(table.at[:, k * 256:(k + 1) * 256], acc.at[k, :384, :], 5 + k) for k in range(8)
    ]
    tok_copy = load(tokens, tok, 1)
    targets_copy = load(targets, target, 0)

    barrier = pltpu.get_barrier_semaphore()
    partners = [near(a, s) for a in "xzy" for s in (1, -1)] + [near("x", 2), near("z", 2), peer]
    for device in partners:
        pl.semaphore_signal(barrier, inc=1, device_id=device, device_id_type=MESH)
    pl.semaphore_wait(barrier, len(partners))

    class Scatter:
        def __init__(self, axis, piece, first, second):
            self.axis, self.piece, self.first, self.second = axis, piece, first, second
            self.r = rank[axis]
            self.above, self.below = mod4(self.r + 1), mod4(self.r - 1)
            self.up, self.down = near(axis, 1), near(axis, -1)

        def far(self):
            far = mod4(self.r + 2)
            self.far_up = send(self.piece(far, 0), self.first.at[0], self.up)
            self.far_down = send(self.piece(far, 1), self.first.at[1], self.down)

        def direct_up(self):
            self.own_up = send(self.piece(self.above, 1), self.second.at[0, 1], self.up)

        def direct_down(self):
            self.own_down = send(self.piece(self.below, 0), self.second.at[1, 0], self.down)

        def direct(self):
            self.direct_up()
            self.direct_down()

        def add(self, p, h, more):
            ref = self.piece(p, h)
            ref[...] = (ref[...].astype(F32) + more[...].astype(F32)).astype(ref.dtype)
            return ref

        def relay_up(self):
            self.far_up.wait_recv()
            ref = self.add(self.above, 0, self.first.at[0])
            self.sum_up = send(ref, self.second.at[0, 0], self.up)

        def relay_down(self):
            self.far_down.wait_recv()
            ref = self.add(self.below, 1, self.first.at[1])
            self.sum_down = send(ref, self.second.at[1, 1], self.down)

        def relay(self):
            self.relay_up()
            self.relay_down()

        def arrived(self):
            self.sum_up.wait_recv()
            self.own_down.wait_recv()
            self.own_up.wait_recv()
            self.sum_down.wait_recv()

        def total(self, h):
            return (
                self.piece(self.r, h)[...].astype(F32)
                + self.second[0, h].astype(F32)
                + self.second[1, h].astype(F32)
            )

    class DirectScatter:
        def __init__(self, axis, piece, land):
            self.axis, self.piece, self.land = axis, piece, land
            self.r = rank[axis]
            self.sent = []

        def start(self, step):
            src = self.piece(mod4(self.r + step))
            self.sent.append(send(src, self.land.at[len(self.sent)], near(self.axis, step)))

        def total(self):
            for copy in self.sent:
                copy.wait_recv()
            value = self.piece(self.r)[...].astype(F32)
            for i in range(3):
                value += self.land[i].astype(F32)
            return value.astype(BF16)

    class DirectGather:
        def __init__(self, axis, place):
            own = place(rank[axis])
            self.sent = {step: send(own, own, near(axis, step)) for step in (1, -1, 2)}

        def arrived(self, step):
            self.sent[step].wait_recv()

    class Gather:
        def __init__(self, axis, place):
            self.axis, self.place = axis, place
            self.r = rank[axis]

        def start(self):
            own = self.place(self.r, None)
            self.up = send(own, own, near(self.axis, 1))
            self.down = send(own, own, near(self.axis, -1))

        def relay_up(self):
            self.up.wait_recv()
            ref = self.place(mod4(self.r - 1), 0)
            self.next_up = send(ref, ref, near(self.axis, 1))

        def relay_down(self):
            self.down.wait_recv()
            ref = self.place(mod4(self.r + 1), 1)
            self.next_down = send(ref, ref, near(self.axis, -1))

        def relay(self):
            self.relay_up()
            self.relay_down()

        def finish(self):
            self.next_up.wait_recv()
            self.next_down.wait_recv()

    def plane_all_reduce(n, result, fill):
        phase.append(n)
        halves = range(2)
        axes = (("x", "z"), ("z", "x"))

        def blocks_of(half):
            r = rank[axes[half][1]]
            return [mod4(r + 2), mod4(r + 1), mod4(r - 1), r]

        outer = [[], []]
        inner = []
        for half, (a, b) in enumerate(axes):
            for i, block in enumerate(blocks_of(half)):
                def piece(p, h=None, half=half, block=block):
                    if h is None:
                        return sums.at[n, p, rows_at(half * 512 + block * 128, 128), :]
                    return sums.at[n, p, rows_at(half * 512 + block * 128 + h * 64, 64), :]
                if i < RELAYED:
                    outer[half].append(Scatter(a, piece, rs1.at[n, half, i], rs2.at[n, half, i]))
                else:
                    outer[half].append(DirectScatter(a, piece, rs3.at[n, half, i - RELAYED]))
            def piece(p, half=half):
                return half_sums.at[n, half, rows_at(p * 128, 128), :]
            inner.append(DirectScatter(b, piece, land.at[n, half]))

        def finish(half, i):
            one = outer[half][i]
            block = blocks_of(half)[i]
            if i < RELAYED:
                one.arrived()
                for h in range(2):
                    half_sums[n, half, rows_at(block * 128 + h * 64, 64), :] = (
                        one.total(h).astype(BF16)
                    )
            else:
                half_sums[n, half, rows_at(block * 128, 128), :] = one.total()

        for i in range(RELAYED):
            for half in halves:
                outer[half][i].far()
            if i >= 1:
                for half in halves:
                    outer[half][i - 1].direct()
        for half in halves:
            outer[half][RELAYED - 1].direct()
        for i in range(RELAYED, 4):
            for step in (2, 1, -1):
                for half in halves:
                    outer[half][i].start(step)
        fill()
        for half in halves:
            outer[half][0].relay()
        fill()
        for half in halves:
            outer[half][1].relay()
        for i, step in enumerate((2, 1, -1)):
            for half in halves:
                finish(half, i)
                inner[half].start(step)
            if i < 2:
                fill()
        for half in halves:
            finish(half, 3)

        inner_gather = []
        outer_gather = [[], []]

        def hand_over(half, p, block):
            ref = result.at[c * 4 + p, half * 4 + block]
            pltpu.make_async_remote_copy(
                src_ref=ref, dst_ref=ref, send_sem=across_send.at[n], recv_sem=across_recv.at[n],
                device_id=peer, device_id_type=MESH,
            ).start()

        def spread(half, block):
            a = axes[half][0]
            def place(p, h=None):
                if h is None:
                    return result.at[c * 4 + p, half * 4 + block]
                return result.at[c * 4 + p, half * 4 + block, pl.ds(h * 64, 64), :]
            if len(outer_gather[half]) < 3:
                g = Gather(a, place)
                g.start()
            else:
                g = DirectGather(a, place)
            outer_gather[half].append((g, block))
            hand_over(half, rank[a], block)

        for half, (a, b) in enumerate(axes):
            chunk = c * 4 + rank[a]
            result[chunk, half * 4 + rank[b]] = inner[half].total()
            def place(p, half=half, chunk=chunk):
                return result.at[chunk, half * 4 + p]
            inner_gather.append(DirectGather(b, place))
            spread(half, rank[b])

        def spread_relay(half, i):
            g, block = outer_gather[half][i]
            r = rank[axes[half][0]]
            if i < 3:
                g.relay_up()
            else:
                g.arrived(1)
            hand_over(half, mod4(r - 1), block)
            if i < 3:
                g.relay_down()
            else:
                g.arrived(-1)
            hand_over(half, mod4(r + 1), block)

        def spread_finish(half, i):
            g, block = outer_gather[half][i]
            if i < 3:
                g.finish()
            else:
                g.arrived(2)
            hand_over(half, mod4(rank[axes[half][0]] + 2), block)

        for half in halves:
            r = rank[axes[half][1]]
            inner_gather[half].arrived(1)
            spread(half, mod4(r - 1))
            inner_gather[half].arrived(-1)
            spread(half, mod4(r + 1))
        fill()
        for half in halves:
            spread_relay(half, 0)
        fill()
        for half in halves:
            inner_gather[half].arrived(2)
            spread(half, mod4(rank[axes[half][1]] + 2))
        fill()
        for half in halves:
            spread_relay(half, 1)
            spread_relay(half, 2)
        fill()
        for half in halves:
            spread_finish(half, 0)
        for half in halves:
            spread_relay(half, 3)
        for half in halves:
            for i in range(1, 4):
                spread_finish(half, i)
        across = pltpu.make_async_remote_copy(
            src_ref=result.at[pl.ds(c * 4, 4)], dst_ref=result.at[pl.ds((1 - c) * 4, 4)],
            send_sem=across_send.at[n], recv_sem=across_recv.at[n],
            device_id=peer, device_id_type=MESH,
        )
        across.wait_send()
        across.wait_recv()
        bytes_sent = tok.at[pl.ds(0, 960), :]
        pltpu.make_async_remote_copy(
            src_ref=bytes_sent, dst_ref=bytes_sent, send_sem=plane_send.at[n],
            recv_sem=plane_send.at[n], device_id=peer, device_id_type=MESH,
        ).wait_send()
        phase.pop()

    for copy in tab_copies:
        copy.wait()
    for k in range(4):
        for j in range(3):
            tab_send[j, k] = acc[(1 - c) * 4 + k, j * BLOCK:(j + 1) * BLOCK, :].astype(BF16)
    table_half = send(tab_send, tab6.at[pl.ds(c * 3, 3)], peer)
    for k in range(4):
        for j in range(3):
            tab6[c * 3 + j, k] = acc[c * 4 + k, j * BLOCK:(j + 1) * BLOCK, :].astype(BF16)
    table_half.wait_recv()
    for b in range(8):
        block = ids[b]
        owner = block // 3
        owner_dp = owner // 4
        here = jnp.logical_and(lax.rem(owner, 4) == z, owner_dp // 2 == x)
        slot = lax.rem(owner_dp, 2) * 3 + lax.rem(block, 3)
        for k in range(4):
            sums[0, k, b * BLOCK:(b + 1) * BLOCK, :] = jnp.where(
                here, tab6[slot, k].astype(F32), 0.0
            ).astype(BF16)
    plane_all_reduce(0, rows, lambda: None)

    tok_copy.wait()
    targets_copy.wait()

    def logits_of(p):
        @pl.loop(0, 4)
        def _(n):
            total = jnp.zeros((256, 256), F32)
            for k in range(8):
                total += lax.dot_general(
                    tok[rows_at(p * 256, 256), k * 256:(k + 1) * 256],
                    rows[k, pl.ds(n * 2, 2)].reshape(256, 256),
                    (((1,), (1,)), ((), ())),
                    preferred_element_type=F32,
                )
            part[rows_at(p * 256, 256), pl.ds(pl.multiple_of(n * 256, 256), 256)] = total * SCALE

    def encode(start):
        @pl.loop(0, 4)
        def _(t):
            some = rows_at(start + t * 16, 16)
            value = part[some, :]
            peak = jnp.max(jnp.abs(value), axis=1, keepdims=True)
            power = jnp.ceil(jnp.log(jnp.maximum(peak, 1e-18)) * LOG_STEP)
            steps = value * (jnp.exp(power * (-1.0 / LOG_STEP)) * STEPS)
            wire[some, :1024] = jnp.round(steps).astype(jnp.int32).astype(WIRE)
            wire[some, 1024:] = jnp.broadcast_to(power, (16, 128)).astype(jnp.int32).astype(WIRE)

    def decode(message):
        power = message[:, 1024:].astype(F32)[:, :1]
        return message[:, :1024].astype(F32) * (jnp.exp(power * (1.0 / LOG_STEP)) * (1.0 / STEPS))

    class LogitScatter(Scatter):
        def __init__(self, u):
            self.u = u
            super().__init__("y", self.encoded, y1.at[u], y2.at[u])

        def start(self, p, h):
            return pl.multiple_of(p * 256 + self.u * 128 + h * 64, 64)

        def encoded(self, p, h):
            encode(self.start(p, h))
            return wire.at[rows_at(self.start(p, h), 64), :]

        def add(self, p, h, more):
            @pl.loop(0, 4)
            def _(t):
                part[rows_at(self.start(p, h) + t * 16, 16), :] += decode(more[rows_at(t * 16, 16), :])
            return self.encoded(p, h)

    parts = [LogitScatter(u) for u in range(2)]
    logits_of(mod4(y + 2))
    parts[0].far()
    parts[1].far()
    logits_of(mod4(y + 1))
    parts[0].direct_up()
    logits_of(mod4(y - 1))
    parts[0].direct_down()
    parts[0].relay()
    parts[1].direct()
    logits_of(y)
    parts[1].relay()

    gathers = []
    for u in range(2):
        parts[u].arrived()
        line = target[pl.ds(y * 2 + u, 1), :].astype(F32)
        column[...] = jnp.transpose(jnp.broadcast_to(line, (128, 128)))

        @pl.loop(0, 4)
        def _(t):
            h, some = t // 2, rows_at(lax.rem(t, 2) * 32, 32)
            logits = (
                part[rows_at(y * 256 + u * 128 + t * 32, 32), :]
                + decode(y2[u, 0, h, some, :])
                + decode(y2[u, 1, h, some, :])
            )
            exponent = jnp.exp(logits - jnp.max(logits, axis=1, keepdims=True))
            probability = exponent * (1.0 / jnp.sum(exponent, axis=1, keepdims=True))
            place = lax.broadcasted_iota(jnp.int32, (32, 1024), 1).astype(F32)
            onehot = jnp.where(column[rows_at(t * 32, 32), :1] == place, 1.0, 0.0)
            dl[rows_at(y * 256 + u * 128 + t * 32, 32), :] = (probability - onehot).astype(BF16)

        def dl_place(p, h, u=u):
            if h is None:
                return dl.at[rows_at(p * 256 + u * 128, 128), :]
            return dl.at[rows_at(p * 256 + u * 128 + h * 64, 64), :]

        g = Gather("y", dl_place)
        g.start()
        gathers.append(g)
    gathers[0].relay()

    def turn(p):
        dl_t[p] = jnp.transpose(dl[rows_at(p * 256, 256), :])

    def product(p, k, n):
        return jnp.dot(
            dl_t[p, rows_at(n * 512, 512), :],
            tok[rows_at(p * 256, 256), pl.ds(pl.multiple_of(k * 256, 256), 256)],
            preferred_element_type=F32,
        )

    def each_tile(f):
        @pl.loop(0, 8)
        def _(k):
            @pl.loop(0, 2)
            def _(n):
                f(k, n)

    turn(y)

    def first(k, n):
        acc[k, rows_at(n * 512, 512), :] = product(y, k, n)

    each_tile(first)
    gathers[1].relay()
    up, down, far = mod4(y + 1), mod4(y - 1), mod4(y + 2)
    turn(up)
    turn(down)

    def second(k, n):
        acc[k, rows_at(n * 512, 512), :] += product(up, k, n) + product(down, k, n)

    each_tile(second)
    for g in gathers:
        g.finish()
    turn(far)

    g_send = sums.at[0]
    crossing = []
    for q in range(4):
        k = (1 - c) * 4 + q
        @pl.loop(0, 2)
        def _(n):
            here = rows_at(n * 512, 512)
            g_send[q, here, :] = ((acc[k, here, :] + product(far, k, n)) * SCALE).astype(BF16)
        crossing.append(send(g_send.at[q], g_recv.at[q], peer))
    for q in range(4):
        k = c * 4 + q
        crossing[q].wait_recv()
        @pl.loop(0, 2)
        def _(n):
            here = rows_at(n * 512, 512)
            total = (acc[k, here, :] + product(far, k, n)) * SCALE
            sums[1, q, here, :] = (total + g_recv[q, here, :].astype(F32)).astype(BF16)
    chunks = iter(range(8))

    def token_chunk():
        k = next(chunks)

        @pl.loop(0, 2)
        def _(n):
            here = rows_at(n * 512, 512)
            tok[here, k * 256:(k + 1) * 256] = (
                jnp.dot(dl[here, :], rows[k].reshape(1024, 256), preferred_element_type=F32) * SCALE
            ).astype(BF16)

    plane_all_reduce(1, grad, token_chunk)
    assert next(chunks, None) is None
    tok_out_copy = load(tok, tok_out, 2)
    for j in range(3):
        place = 0
        for b in range(8):
            place += b * (ids[b] == (dp * 4 + z) * 3 + j).astype(jnp.int32)
        place = jnp.minimum(place, 7)
        for k in range(8):
            picked[j * BLOCK:(j + 1) * BLOCK, k * 256:(k + 1) * 256] = grad[k, place]
    grad_copy = load(picked, grad_out, 3)

    assert (len(pending), len(landed)) == (N_SEND, N_RECV), (len(pending), len(landed))
    for copy in pending:
        copy.wait_send()
    tok_out_copy.wait()
    grad_copy.wait()


def communicate(ids, tokens, table, targets):
    vmem = pltpu.VMEM
    return pl.pallas_call(
        comm_kernel,
        out_shape=(
            jax.ShapeDtypeStruct((1024, 2048), BF16),
            jax.ShapeDtypeStruct((384, 2048), BF16),
        ),
        in_specs=[
            pl.BlockSpec(memory_space=pltpu.SMEM),
            pl.BlockSpec(memory_space=pltpu.HBM),
            pl.BlockSpec(memory_space=pltpu.HBM),
            pl.BlockSpec(memory_space=pltpu.HBM),
        ],
        out_specs=(pl.BlockSpec(memory_space=pl.ANY),) * 2,
        scratch_shapes=[
            vmem((1024, 2048), BF16),
            vmem((8, 128), jnp.int32),
            vmem((6, 4, 128, 256), BF16),
            vmem((3, 4, 128, 256), BF16),
            vmem((8, 8, 128, 256), BF16),
            vmem((1024, 1024), F32),
            vmem((1024, 1152), WIRE),
            vmem((1024, 1024), BF16),
            vmem((4, 1024, 256), BF16),
            vmem((8, 1024, 256), F32),
            vmem((4, 1024, 256), BF16),
            vmem((8, 8, 128, 256), BF16),
            vmem((384, 2048), BF16),
            vmem((2, 4, 1024, 256), BF16),
            vmem((2, 2, 512, 256), BF16),
            vmem((2, 2, RELAYED, 2, 64, 256), BF16),
            vmem((2, 2, RELAYED, 2, 2, 64, 256), BF16),
            vmem((2, 2, 4 - RELAYED, 3, 128, 256), BF16),
            vmem((2, 2, 3, 128, 256), BF16),
            vmem((2, 2, 64, 1152), WIRE),
            vmem((2, 2, 2, 64, 1152), WIRE),
            vmem((128, 128), F32),
            pltpu.SemaphoreType.DMA((N_SEND,)),
            pltpu.SemaphoreType.DMA((N_RECV,)),
            pltpu.SemaphoreType.DMA((2,)),
            pltpu.SemaphoreType.DMA((13,)),
            pltpu.SemaphoreType.DMA((2,)),
            pltpu.SemaphoreType.DMA((2,)),
        ],
        compiler_params=pltpu.CompilerParams(
            collective_id=0, has_side_effects=True, vmem_limit_bytes=56 * 2**20
        ),
    )(ids, tokens, table, targets)


def update_kernel(where, grad, w, m, v, tok_in, w_out, m_out, v_out, tok_out):
    tok_out[...] = tok_in[...]
    for j in range(3):
        here = slice(j * BLOCK, (j + 1) * BLOCK)
        listed = where[0] == where[8] + j
        for b in range(1, 8):
            listed = jnp.logical_or(listed, where[b] == where[8] + j)
        old = (w[here, :], m[here, :], v[here, :])
        new = adamw_rows(*old, grad[here, :].astype(F32))
        w_out[here, :] = jnp.where(listed, new[0], old[0])
        m_out[here, :] = jnp.where(listed, new[1], old[1])
        v_out[here, :] = jnp.where(listed, new[2], old[2])


def update(where, grad, table, moment_one, moment_two, token_grads):
    wide = pl.BlockSpec((384, 256), lambda k: (0, k))
    tall = pl.BlockSpec((1024, 256), lambda k: (0, k))
    return pl.pallas_call(
        update_kernel,
        grid=(8,),
        in_specs=[pl.BlockSpec(memory_space=pltpu.SMEM), wide, wide, wide, wide, tall],
        out_specs=[wide, wide, wide, tall],
        out_shape=[jax.ShapeDtypeStruct((384, 2048), F32)] * 3
        + [jax.ShapeDtypeStruct((1024, 2048), BF16)],
        compiler_params=pltpu.CompilerParams(vmem_limit_bytes=47 * 2**20),
    )(where, grad, table, moment_one, moment_two, token_grads)


def body(tokens, table, moment_one, moment_two, block_ids, targets):
    owner = lax.axis_index(("dp", "vocab"))
    where = jnp.concatenate([block_ids, jnp.reshape(owner * 3, (1,)).astype(jnp.int32)])
    token_grads, grad = communicate(where, tokens, table, targets.reshape(8, 128))
    return tuple(update(where, grad, table, moment_one, moment_two, token_grads))


def solution(mesh):
    wide = P(("dp", "vocab"), "width")
    return jax.shard_map(
        body,
        mesh=mesh,
        in_specs=(wide, wide, wide, wide, P(), P(("dp", "vocab"))),
        out_specs=(wide, wide, wide, wide),
        check_vma=False,
    )
```

```python
import functools
import math

import jax
import jax.numpy as jnp
from jax import lax
from jax.experimental import pallas as pl
from jax.experimental.pallas import tpu as pltpu
from jax.sharding import PartitionSpec as P

D = 8192
BLOCK = 128
SCALE = 1.0 / math.sqrt(D)
MESH = pl.DeviceIdType.MESH
BF16 = jnp.bfloat16
F32 = jnp.float32
WIRE = jnp.int16
STEPS = 32700.0
LOG_STEP = 256.0

beta_one = 0.9
beta_two = 0.95
learn_rate = 0.01
decay_rate = 0.1
epsilon = 1e-08

RELAYED = 2
STEPS_UPDATE = 4
N_SEND = 25
N_RECV = 181


def adamw_rows(weights, first, second, grads):
    first_new = beta_one * first + (1.0 - beta_one) * grads
    second_new = beta_two * second + (1.0 - beta_two) * grads * grads
    correct_one = 1.0 - beta_one**10
    correct_two = 1.0 - beta_two**10
    squared = second_new * (1.0 / correct_two)
    update = (
        first_new * (1.0 / correct_one) / (squared * lax.rsqrt(squared) + epsilon)
        + decay_rate * weights
    )
    return (weights - learn_rate * update, first_new, second_new)


def mod4(v):
    return lax.rem(v + 4, 4)


def rows_at(start, size):
    return pl.ds(pl.multiple_of(start, size), size)


def comm_kernel(
    ids, tokens, table, targets,
    tok_out, grad_out,
    tok, target, tab6, tab_send, rows, part, wire, dl, dl_t, acc, g_recv, grad, picked,
    sums, half_sums, rs1, rs2, rs3, land, y1, y2, column,
    send_sem, recv_sem, plane_send, local_sem, across_send, across_recv,
):
    dp = lax.axis_index("dp")
    z = lax.axis_index("vocab")
    y = lax.axis_index("width")
    x = dp // 2
    c = lax.rem(dp, 2)
    rank = {"x": x, "z": z, "y": y}
    pending = []

    def near(axis, step):
        if axis == "x":
            return (mod4(x + step) * 2 + c, z, y)
        if axis == "z":
            return (dp, mod4(z + step), y)
        return (dp, z, mod4(y + step))

    peer = (x * 2 + (1 - c), z, y)

    landed = []
    phase = []

    def send(src, dst, device):
        left = plane_send.at[phase[0]] if phase else send_sem.at[len(pending)]
        copy = pltpu.make_async_remote_copy(
            src_ref=src, dst_ref=dst, send_sem=left, recv_sem=recv_sem.at[len(landed)],
            device_id=device, device_id_type=MESH,
        )
        copy.start()
        landed.append(copy)
        if not phase:
            pending.append(copy)
        return copy

    def load(src, dst, i):
        copy = pltpu.make_async_copy(src, dst, local_sem.at[i])
        copy.start()
        return copy

    tab_copies = [
        load(table.at[:, k * 256:(k + 1) * 256], acc.at[k, :384, :], 5 + k) for k in range(8)
    ]
    tok_copy = load(tokens, tok, 1)
    targets_copy = load(targets, target, 0)

    barrier = pltpu.get_barrier_semaphore()
    partners = [near(a, s) for a in "xzy" for s in (1, -1)] + [near("x", 2), near("z", 2), peer]
    for device in partners:
        pl.semaphore_signal(barrier, inc=1, device_id=device, device_id_type=MESH)

    for copy in tab_copies:
        copy.wait()
    for k in range(4):
        for j in range(3):
            tab_send[j, k] = acc[(1 - c) * 4 + k, j * BLOCK:(j + 1) * BLOCK, :].astype(BF16)
    for k in range(4):
        for j in range(3):
            tab6[c * 3 + j, k] = acc[c * 4 + k, j * BLOCK:(j + 1) * BLOCK, :].astype(BF16)
    pl.semaphore_wait(barrier, len(partners))

    class Scatter:
        def __init__(self, axis, piece, first, second):
            self.axis, self.piece, self.first, self.second = axis, piece, first, second
            self.r = rank[axis]
            self.above, self.below = mod4(self.r + 1), mod4(self.r - 1)
            self.up, self.down = near(axis, 1), near(axis, -1)

        def far(self):
            far = mod4(self.r + 2)
            self.far_up = send(self.piece(far, 0), self.first.at[0], self.up)
            self.far_down = send(self.piece(far, 1), self.first.at[1], self.down)

        def direct_up(self):
            self.own_up = send(self.piece(self.above, 1), self.second.at[0, 1], self.up)

        def direct_down(self):
            self.own_down = send(self.piece(self.below, 0), self.second.at[1, 0], self.down)

        def direct(self):
            self.direct_up()
            self.direct_down()

        def add(self, p, h, more):
            ref = self.piece(p, h)
            ref[...] = (ref[...].astype(F32) + more[...].astype(F32)).astype(ref.dtype)
            return ref

        def relay_up(self):
            self.far_up.wait_recv()
            ref = self.add(self.above, 0, self.first.at[0])
            self.sum_up = send(ref, self.second.at[0, 0], self.up)

        def relay_down(self):
            self.far_down.wait_recv()
            ref = self.add(self.below, 1, self.first.at[1])
            self.sum_down = send(ref, self.second.at[1, 1], self.down)

        def relay(self):
            self.relay_up()
            self.relay_down()

        def arrived(self):
            self.sum_up.wait_recv()
            self.own_down.wait_recv()
            self.own_up.wait_recv()
            self.sum_down.wait_recv()

        def total(self, h):
            return (
                self.piece(self.r, h)[...].astype(F32)
                + self.second[0, h].astype(F32)
                + self.second[1, h].astype(F32)
            )

    class DirectScatter:
        def __init__(self, axis, piece, land):
            self.axis, self.piece, self.land = axis, piece, land
            self.r = rank[axis]
            self.sent = []

        def start(self, step):
            src = self.piece(mod4(self.r + step))
            self.sent.append(send(src, self.land.at[len(self.sent)], near(self.axis, step)))

        def total(self):
            for copy in self.sent:
                copy.wait_recv()
            value = self.piece(self.r)[...].astype(F32)
            for i in range(3):
                value += self.land[i].astype(F32)
            return value.astype(BF16)

    class DirectGather:
        def __init__(self, axis, place):
            own = place(rank[axis])
            self.sent = {step: send(own, own, near(axis, step)) for step in (1, -1, 2)}

        def arrived(self, step):
            self.sent[step].wait_recv()

    class Gather:
        def __init__(self, axis, place):
            self.axis, self.place = axis, place
            self.r = rank[axis]

        def start(self):
            own = self.place(self.r, None)
            self.up = send(own, own, near(self.axis, 1))
            self.down = send(own, own, near(self.axis, -1))

        def relay_up(self):
            self.up.wait_recv()
            ref = self.place(mod4(self.r - 1), 0)
            self.next_up = send(ref, ref, near(self.axis, 1))

        def relay_down(self):
            self.down.wait_recv()
            ref = self.place(mod4(self.r + 1), 1)
            self.next_down = send(ref, ref, near(self.axis, -1))

        def relay(self):
            self.relay_up()
            self.relay_down()

        def finish(self):
            self.next_up.wait_recv()
            self.next_down.wait_recv()

    def plane_all_reduce(n, result, fill):
        phase.append(n)
        halves = range(2)
        axes = (("x", "z"), ("z", "x"))

        def blocks_of(half):
            r = rank[axes[half][1]]
            return [mod4(r + 2), mod4(r + 1), mod4(r - 1), r]

        outer = [[], []]
        inner = []
        for half, (a, b) in enumerate(axes):
            for i, block in enumerate(blocks_of(half)):
                def piece(p, h=None, half=half, block=block):
                    if h is None:
                        return sums.at[n, p, rows_at(half * 512 + block * 128, 128), :]
                    return sums.at[n, p, rows_at(half * 512 + block * 128 + h * 64, 64), :]
                if i < RELAYED:
                    outer[half].append(Scatter(a, piece, rs1.at[n, half, i], rs2.at[n, half, i]))
                else:
                    outer[half].append(DirectScatter(a, piece, rs3.at[n, half, i - RELAYED]))
            def piece(p, half=half):
                return half_sums.at[n, half, rows_at(p * 128, 128), :]
            inner.append(DirectScatter(b, piece, land.at[n, half]))

        def finish(half, i):
            one = outer[half][i]
            block = blocks_of(half)[i]
            if i < RELAYED:
                one.arrived()
                for h in range(2):
                    half_sums[n, half, rows_at(block * 128 + h * 64, 64), :] = (
                        one.total(h).astype(BF16)
                    )
            else:
                half_sums[n, half, rows_at(block * 128, 128), :] = one.total()

        for i in range(RELAYED):
            for half in halves:
                outer[half][i].far()
            if i >= 1:
                for half in halves:
                    outer[half][i - 1].direct()
        for half in halves:
            outer[half][RELAYED - 1].direct()
        for i in range(RELAYED, 4):
            for step in (2, 1, -1):
                for half in halves:
                    outer[half][i].start(step)
        fill()
        for half in halves:
            outer[half][0].relay()
        fill()
        for half in halves:
            outer[half][1].relay()
        for i, step in enumerate((2, 1, -1)):
            for half in halves:
                finish(half, i)
                inner[half].start(step)
            if i < 2:
                fill()
        for half in halves:
            finish(half, 3)

        inner_gather = []
        outer_gather = [[], []]

        def hand_over(half, p, block):
            ref = result.at[c * 4 + p, half * 4 + block]
            pltpu.make_async_remote_copy(
                src_ref=ref, dst_ref=ref, send_sem=across_send.at[n], recv_sem=across_recv.at[n],
                device_id=peer, device_id_type=MESH,
            ).start()

        def spread(half, block):
            a = axes[half][0]
            def place(p, h=None):
                if h is None:
                    return result.at[c * 4 + p, half * 4 + block]
                return result.at[c * 4 + p, half * 4 + block, pl.ds(h * 64, 64), :]
            if len(outer_gather[half]) < 3:
                g = Gather(a, place)
                g.start()
            else:
                g = DirectGather(a, place)
            outer_gather[half].append((g, block))
            hand_over(half, rank[a], block)

        for half, (a, b) in enumerate(axes):
            chunk = c * 4 + rank[a]
            result[chunk, half * 4 + rank[b]] = inner[half].total()
            def place(p, half=half, chunk=chunk):
                return result.at[chunk, half * 4 + p]
            inner_gather.append(DirectGather(b, place))
            spread(half, rank[b])

        def spread_relay(half, i):
            g, block = outer_gather[half][i]
            r = rank[axes[half][0]]
            if i < 3:
                g.relay_up()
            else:
                g.arrived(1)
            hand_over(half, mod4(r - 1), block)
            if i < 3:
                g.relay_down()
            else:
                g.arrived(-1)
            hand_over(half, mod4(r + 1), block)

        def spread_finish(half, i):
            g, block = outer_gather[half][i]
            if i < 3:
                g.finish()
            else:
                g.arrived(2)
            hand_over(half, mod4(rank[axes[half][0]] + 2), block)

        for half in halves:
            r = rank[axes[half][1]]
            inner_gather[half].arrived(1)
            spread(half, mod4(r - 1))
            inner_gather[half].arrived(-1)
            spread(half, mod4(r + 1))
        fill()
        for half in halves:
            spread_relay(half, 0)
        fill()
        for half in halves:
            inner_gather[half].arrived(2)
            spread(half, mod4(rank[axes[half][1]] + 2))
        fill()
        for half in halves:
            spread_relay(half, 1)
            spread_relay(half, 2)
        fill()
        for half in halves:
            spread_finish(half, 0)
        for half in halves:
            spread_relay(half, 3)
        for half in halves:
            for i in range(1, 4):
                spread_finish(half, i)
        across = pltpu.make_async_remote_copy(
            src_ref=result.at[pl.ds(c * 4, 4)], dst_ref=result.at[pl.ds((1 - c) * 4, 4)],
            send_sem=across_send.at[n], recv_sem=across_recv.at[n],
            device_id=peer, device_id_type=MESH,
        )
        across.wait_send()
        across.wait_recv()
        bytes_sent = tok.at[pl.ds(0, 960), :]
        pltpu.make_async_remote_copy(
            src_ref=bytes_sent, dst_ref=bytes_sent, send_sem=plane_send.at[n],
            recv_sem=plane_send.at[n], device_id=peer, device_id_type=MESH,
        ).wait_send()
        phase.pop()

    table_half = send(tab_send, tab6.at[pl.ds(c * 3, 3)], peer)
    table_half.wait_recv()
    for b in range(8):
        block = ids[b]
        owner = block // 3
        owner_dp = owner // 4
        here = jnp.logical_and(lax.rem(owner, 4) == z, owner_dp // 2 == x)
        slot = lax.rem(owner_dp, 2) * 3 + lax.rem(block, 3)
        for k in range(4):
            sums[0, k, b * BLOCK:(b + 1) * BLOCK, :] = jnp.where(
                here, tab6[slot, k].astype(F32), 0.0
            ).astype(BF16)
    plane_all_reduce(0, rows, lambda: None)

    tok_copy.wait()
    targets_copy.wait()

    def logits_of(p):
        @pl.loop(0, 4)
        def _(n):
            total = jnp.zeros((256, 256), F32)
            for k in range(8):
                total += lax.dot_general(
                    tok[rows_at(p * 256, 256), k * 256:(k + 1) * 256],
                    rows[k, pl.ds(n * 2, 2)].reshape(256, 256),
                    (((1,), (1,)), ((), ())),
                    preferred_element_type=F32,
                )
            part[rows_at(p * 256, 256), pl.ds(pl.multiple_of(n * 256, 256), 256)] = total * SCALE

    def encode(start):
        @pl.loop(0, 4)
        def _(t):
            some = rows_at(start + t * 16, 16)
            value = part[some, :]
            peak = jnp.max(jnp.abs(value), axis=1, keepdims=True)
            power = jnp.ceil(jnp.log(jnp.maximum(peak, 1e-18)) * LOG_STEP)
            steps = value * (jnp.exp(power * (-1.0 / LOG_STEP)) * STEPS)
            wire[some, :1024] = jnp.round(steps).astype(jnp.int32).astype(WIRE)
            wire[some, 1024:] = jnp.broadcast_to(power, (16, 128)).astype(jnp.int32).astype(WIRE)

    def decode(message):
        power = message[:, 1024:].astype(F32)[:, :1]
        return message[:, :1024].astype(F32) * (jnp.exp(power * (1.0 / LOG_STEP)) * (1.0 / STEPS))

    class LogitScatter(Scatter):
        def __init__(self, u):
            self.u = u
            super().__init__("y", self.encoded, y1.at[u], y2.at[u])

        def start(self, p, h):
            return pl.multiple_of(p * 256 + self.u * 128 + h * 64, 64)

        def encoded(self, p, h):
            encode(self.start(p, h))
            return wire.at[rows_at(self.start(p, h), 64), :]

        def add(self, p, h, more):
            @pl.loop(0, 4)
            def _(t):
                part[rows_at(self.start(p, h) + t * 16, 16), :] += decode(more[rows_at(t * 16, 16), :])
            return self.encoded(p, h)

    parts = [LogitScatter(u) for u in range(2)]
    logits_of(mod4(y + 2))
    parts[0].far()
    parts[1].far()
    logits_of(mod4(y + 1))
    parts[0].direct_up()
    logits_of(mod4(y - 1))
    parts[0].direct_down()
    parts[0].relay()
    parts[1].direct()
    logits_of(y)
    parts[1].relay()

    gathers = []
    for u in range(2):
        parts[u].arrived()
        line = target[pl.ds(y * 2 + u, 1), :].astype(F32)
        column[...] = jnp.transpose(jnp.broadcast_to(line, (128, 128)))

        @pl.loop(0, 4)
        def _(t):
            h, some = t // 2, rows_at(lax.rem(t, 2) * 32, 32)
            logits = (
                part[rows_at(y * 256 + u * 128 + t * 32, 32), :]
                + decode(y2[u, 0, h, some, :])
                + decode(y2[u, 1, h, some, :])
            )
            exponent = jnp.exp(logits - jnp.max(logits, axis=1, keepdims=True))
            probability = exponent * (1.0 / jnp.sum(exponent, axis=1, keepdims=True))
            place = lax.broadcasted_iota(jnp.int32, (32, 1024), 1).astype(F32)
            onehot = jnp.where(column[rows_at(t * 32, 32), :1] == place, 1.0, 0.0)
            dl[rows_at(y * 256 + u * 128 + t * 32, 32), :] = (probability - onehot).astype(BF16)

        def dl_place(p, h, u=u):
            if h is None:
                return dl.at[rows_at(p * 256 + u * 128, 128), :]
            return dl.at[rows_at(p * 256 + u * 128 + h * 64, 64), :]

        g = Gather("y", dl_place)
        g.start()
        gathers.append(g)
    gathers[0].relay()

    def turn(p):
        dl_t[p] = jnp.transpose(dl[rows_at(p * 256, 256), :])

    def product(p, k, n):
        return jnp.dot(
            dl_t[p, rows_at(n * 512, 512), :],
            tok[rows_at(p * 256, 256), pl.ds(pl.multiple_of(k * 256, 256), 256)],
            preferred_element_type=F32,
        )

    def each_tile(f):
        @pl.loop(0, 8)
        def _(k):
            @pl.loop(0, 2)
            def _(n):
                f(k, n)

    turn(y)

    def first(k, n):
        acc[k, rows_at(n * 512, 512), :] = product(y, k, n)

    each_tile(first)
    gathers[1].relay()
    up, down, far = mod4(y + 1), mod4(y - 1), mod4(y + 2)
    turn(up)
    turn(down)

    def second(k, n):
        acc[k, rows_at(n * 512, 512), :] += product(up, k, n) + product(down, k, n)

    each_tile(second)
    for g in gathers:
        g.finish()
    turn(far)

    g_send = sums.at[0]
    crossing = []
    for q in range(4):
        k = (1 - c) * 4 + q
        @pl.loop(0, 2)
        def _(n):
            here = rows_at(n * 512, 512)
            g_send[q, here, :] = ((acc[k, here, :] + product(far, k, n)) * SCALE).astype(BF16)
        crossing.append(send(g_send.at[q], g_recv.at[q], peer))
    for q in range(4):
        k = c * 4 + q
        crossing[q].wait_recv()
        @pl.loop(0, 2)
        def _(n):
            here = rows_at(n * 512, 512)
            total = (acc[k, here, :] + product(far, k, n)) * SCALE
            sums[1, q, here, :] = (total + g_recv[q, here, :].astype(F32)).astype(BF16)
    chunks = iter(range(8))

    def token_chunk():
        k = next(chunks)

        @pl.loop(0, 2)
        def _(n):
            here = rows_at(n * 512, 512)
            tok[here, k * 256:(k + 1) * 256] = (
                jnp.dot(dl[here, :], rows[k].reshape(1024, 256), preferred_element_type=F32) * SCALE
            ).astype(BF16)

    plane_all_reduce(1, grad, token_chunk)
    assert next(chunks, None) is None
    tok_out_copy = load(tok, tok_out, 2)
    for j in range(3):
        place = 0
        for b in range(8):
            place += b * (ids[b] == (dp * 4 + z) * 3 + j).astype(jnp.int32)
        place = jnp.minimum(place, 7)
        for k in range(8):
            picked[j * BLOCK:(j + 1) * BLOCK, k * 256:(k + 1) * 256] = grad[k, place]
    grad_copy = load(picked, grad_out, 3)

    assert (len(pending), len(landed)) == (N_SEND, N_RECV), (len(pending), len(landed))
    for copy in pending:
        copy.wait_send()
    tok_out_copy.wait()
    grad_copy.wait()


def communicate(ids, tokens, table, targets):
    vmem = pltpu.VMEM
    return pl.pallas_call(
        comm_kernel,
        out_shape=(
            jax.ShapeDtypeStruct((1024, 2048), BF16),
            jax.ShapeDtypeStruct((384, 2048), BF16),
        ),
        in_specs=[
            pl.BlockSpec(memory_space=pltpu.SMEM),
            pl.BlockSpec(memory_space=pltpu.HBM),
            pl.BlockSpec(memory_space=pltpu.HBM),
            pl.BlockSpec(memory_space=pltpu.HBM),
        ],
        out_specs=(pl.BlockSpec(memory_space=pl.ANY),) * 2,
        scratch_shapes=[
            vmem((1024, 2048), BF16),
            vmem((8, 128), jnp.int32),
            vmem((6, 4, 128, 256), BF16),
            vmem((3, 4, 128, 256), BF16),
            vmem((8, 8, 128, 256), BF16),
            vmem((1024, 1024), F32),
            vmem((1024, 1152), WIRE),
            vmem((1024, 1024), BF16),
            vmem((4, 1024, 256), BF16),
            vmem((8, 1024, 256), F32),
            vmem((4, 1024, 256), BF16),
            vmem((8, 8, 128, 256), BF16),
            vmem((384, 2048), BF16),
            vmem((2, 4, 1024, 256), BF16),
            vmem((2, 2, 512, 256), BF16),
            vmem((2, 2, RELAYED, 2, 64, 256), BF16),
            vmem((2, 2, RELAYED, 2, 2, 64, 256), BF16),
            vmem((2, 2, 4 - RELAYED, 3, 128, 256), BF16),
            vmem((2, 2, 3, 128, 256), BF16),
            vmem((2, 2, 64, 1152), WIRE),
            vmem((2, 2, 2, 64, 1152), WIRE),
            vmem((128, 128), F32),
            pltpu.SemaphoreType.DMA((N_SEND,)),
            pltpu.SemaphoreType.DMA((N_RECV,)),
            pltpu.SemaphoreType.DMA((2,)),
            pltpu.SemaphoreType.DMA((13,)),
            pltpu.SemaphoreType.DMA((2,)),
            pltpu.SemaphoreType.DMA((2,)),
        ],
        compiler_params=pltpu.CompilerParams(
            collective_id=0, has_side_effects=True, vmem_limit_bytes=56 * 2**20
        ),
    )(ids, tokens, table, targets)


def update_kernel(ids, grad, w, m, v, tok_in, w_out, m_out, v_out, tok_out):
    mine = (lax.axis_index('dp') * 4 + lax.axis_index('vocab')) * 3
    size = w.shape[0] // 3
    tok_out[...] = tok_in[...]
    for part in range(3):
        here = slice(part * size, (part + 1) * size)
        block = mine + (pl.program_id(0) * 3 * size + part * size) // BLOCK
        listed = ids[0] == block
        for b in range(1, 8):
            listed = jnp.logical_or(listed, ids[b] == block)
        old = (w[here, :], m[here, :], v[here, :])
        new = adamw_rows(*old, grad[here, :].astype(F32))
        w_out[here, :] = jnp.where(listed, new[0], old[0])
        m_out[here, :] = jnp.where(listed, new[1], old[1])
        v_out[here, :] = jnp.where(listed, new[2], old[2])


def update(ids, grad, table, moment_one, moment_two, token_grads):
    wide = pl.BlockSpec((384 // STEPS_UPDATE, 2048), lambda k: (k, 0))
    tall = pl.BlockSpec((1024 // STEPS_UPDATE, 2048), lambda k: (k, 0))
    return pl.pallas_call(
        update_kernel,
        grid=(STEPS_UPDATE,),
        in_specs=[pl.BlockSpec(memory_space=pltpu.SMEM), wide, wide, wide, wide, tall],
        out_specs=[wide, wide, wide, tall],
        out_shape=[jax.ShapeDtypeStruct((384, 2048), F32)] * 3
        + [jax.ShapeDtypeStruct((1024, 2048), BF16)],
        compiler_params=pltpu.CompilerParams(vmem_limit_bytes=47 * 2**20),
    )(ids, grad, table, moment_one, moment_two, token_grads)


def body(tokens, table, moment_one, moment_two, block_ids, targets):
    token_grads, grad = communicate(block_ids, tokens, table, targets.reshape(8, 128))
    return tuple(update(block_ids, grad, table, moment_one, moment_two, token_grads))


def solution(mesh):
    wide = P(("dp", "vocab"), "width")
    return jax.shard_map(
        body,
        mesh=mesh,
        in_specs=(wide, wide, wide, wide, P(), P(("dp", "vocab"))),
        out_specs=(wide, wide, wide, wide),
        check_vma=False,
    )
```

```python
import functools
import math

import jax
import jax.numpy as jnp
from jax import lax
from jax.experimental import pallas as pl
from jax.experimental.pallas import tpu as pltpu
from jax.sharding import PartitionSpec as P

D = 8192
BLOCK = 128
SCALE = 1.0 / math.sqrt(D)
MESH = pl.DeviceIdType.MESH
BF16 = jnp.bfloat16
F32 = jnp.float32
WIRE = jnp.int16
STEPS = 32700.0
LOG_STEP = 256.0

beta_one = 0.9
beta_two = 0.95
learn_rate = 0.01
decay_rate = 0.1
epsilon = 1e-08

RELAYED = 2
STEPS_UPDATE = 4
N_SEND = 25
N_RECV = 181


def adamw_rows(weights, first, second, grads):
    first_new = beta_one * first + (1.0 - beta_one) * grads
    second_new = beta_two * second + (1.0 - beta_two) * grads * grads
    correct_one = 1.0 - beta_one**10
    correct_two = 1.0 - beta_two**10
    squared = second_new * (1.0 / correct_two)
    update = (
        first_new * (1.0 / correct_one) / (squared * lax.rsqrt(squared) + epsilon)
        + decay_rate * weights
    )
    return (weights - learn_rate * update, first_new, second_new)


def mod4(v):
    return lax.rem(v + 4, 4)


def rows_at(start, size):
    return pl.ds(pl.multiple_of(start, size), size)


def comm_kernel(
    ids, tokens, table, targets,
    tok_out, grad_out,
    tok, target, tab6, tab_send, rows, part, wire, dl, dl_t, acc, g_recv, grad, picked,
    sums, half_sums, rs1, rs2, rs3, land, y1, y2, column,
    send_sem, recv_sem, plane_send, local_sem, across_send, across_recv,
):
    dp = lax.axis_index("dp")
    z = lax.axis_index("vocab")
    y = lax.axis_index("width")
    x = dp // 2
    c = lax.rem(dp, 2)
    rank = {"x": x, "z": z, "y": y}
    pending = []

    def near(axis, step):
        if axis == "x":
            return (mod4(x + step) * 2 + c, z, y)
        if axis == "z":
            return (dp, mod4(z + step), y)
        return (dp, z, mod4(y + step))

    peer = (x * 2 + (1 - c), z, y)

    landed = []
    phase = []

    def send(src, dst, device):
        left = plane_send.at[phase[0]] if phase else send_sem.at[len(pending)]
        copy = pltpu.make_async_remote_copy(
            src_ref=src, dst_ref=dst, send_sem=left, recv_sem=recv_sem.at[len(landed)],
            device_id=device, device_id_type=MESH,
        )
        copy.start()
        landed.append(copy)
        if not phase:
            pending.append(copy)
        return copy

    def load(src, dst, i):
        copy = pltpu.make_async_copy(src, dst, local_sem.at[i])
        copy.start()
        return copy

    tab_copies = [
        load(table.at[:, k * 256:(k + 1) * 256], acc.at[k, :384, :], 5 + k) for k in range(8)
    ]
    tok_copy = load(tokens, tok, 1)
    targets_copy = load(targets, target, 0)

    barrier = pltpu.get_barrier_semaphore()
    partners = [near(a, s) for a in "xzy" for s in (1, -1)] + [near("x", 2), near("z", 2), peer]
    for device in partners:
        pl.semaphore_signal(barrier, inc=1, device_id=device, device_id_type=MESH)

    for copy in tab_copies:
        copy.wait()
    for k in range(4):
        for j in range(3):
            tab_send[j, k] = acc[(1 - c) * 4 + k, j * BLOCK:(j + 1) * BLOCK, :].astype(BF16)
    for k in range(4):
        for j in range(3):
            tab6[c * 3 + j, k] = acc[c * 4 + k, j * BLOCK:(j + 1) * BLOCK, :].astype(BF16)
    pl.semaphore_wait(barrier, len(partners))

    class Scatter:
        def __init__(self, axis, piece, first, second):
            self.axis, self.piece, self.first, self.second = axis, piece, first, second
            self.r = rank[axis]
            self.above, self.below = mod4(self.r + 1), mod4(self.r - 1)
            self.up, self.down = near(axis, 1), near(axis, -1)

        def far(self):
            far = mod4(self.r + 2)
            self.far_up = send(self.piece(far, 0), self.first.at[0], self.up)
            self.far_down = send(self.piece(far, 1), self.first.at[1], self.down)

        def direct_up(self):
            self.own_up = send(self.piece(self.above, 1), self.second.at[0, 1], self.up)

        def direct_down(self):
            self.own_down = send(self.piece(self.below, 0), self.second.at[1, 0], self.down)

        def direct(self):
            self.direct_up()
            self.direct_down()

        def add(self, p, h, more):
            ref = self.piece(p, h)
            ref[...] = (ref[...].astype(F32) + more[...].astype(F32)).astype(ref.dtype)
            return ref

        def relay_up(self):
            self.far_up.wait_recv()
            ref = self.add(self.above, 0, self.first.at[0])
            self.sum_up = send(ref, self.second.at[0, 0], self.up)

        def relay_down(self):
            self.far_down.wait_recv()
            ref = self.add(self.below, 1, self.first.at[1])
            self.sum_down = send(ref, self.second.at[1, 1], self.down)

        def relay(self):
            self.relay_up()
            self.relay_down()

        def arrived(self):
            self.sum_up.wait_recv()
            self.own_down.wait_recv()
            self.own_up.wait_recv()
            self.sum_down.wait_recv()

        def total(self, h):
            return (
                self.piece(self.r, h)[...].astype(F32)
                + self.second[0, h].astype(F32)
                + self.second[1, h].astype(F32)
            )

    class DirectScatter:
        def __init__(self, axis, piece, land):
            self.axis, self.piece, self.land = axis, piece, land
            self.r = rank[axis]
            self.sent = []

        def start(self, step):
            src = self.piece(mod4(self.r + step))
            self.sent.append(send(src, self.land.at[len(self.sent)], near(self.axis, step)))

        def total(self):
            for copy in self.sent:
                copy.wait_recv()
            value = self.piece(self.r)[...].astype(F32)
            for i in range(3):
                value += self.land[i].astype(F32)
            return value.astype(BF16)

    class DirectGather:
        def __init__(self, axis, place):
            own = place(rank[axis])
            self.sent = {step: send(own, own, near(axis, step)) for step in (1, -1, 2)}

        def arrived(self, step):
            self.sent[step].wait_recv()

    class Gather:
        def __init__(self, axis, place):
            self.axis, self.place = axis, place
            self.r = rank[axis]

        def start(self):
            own = self.place(self.r, None)
            self.up = send(own, own, near(self.axis, 1))
            self.down = send(own, own, near(self.axis, -1))

        def relay_up(self):
            self.up.wait_recv()
            ref = self.place(mod4(self.r - 1), 0)
            self.next_up = send(ref, ref, near(self.axis, 1))

        def relay_down(self):
            self.down.wait_recv()
            ref = self.place(mod4(self.r + 1), 1)
            self.next_down = send(ref, ref, near(self.axis, -1))

        def relay(self):
            self.relay_up()
            self.relay_down()

        def finish(self):
            self.next_up.wait_recv()
            self.next_down.wait_recv()

    def plane_all_reduce(n, result, fill):
        phase.append(n)
        halves = range(2)
        axes = (("x", "z"), ("z", "x"))

        def blocks_of(half):
            r = rank[axes[half][1]]
            return [mod4(r + 2), mod4(r + 1), mod4(r - 1), r]

        outer = [[], []]
        inner = []
        for half, (a, b) in enumerate(axes):
            for i, block in enumerate(blocks_of(half)):
                def piece(p, h=None, half=half, block=block):
                    if h is None:
                        return sums.at[n, p, rows_at(half * 512 + block * 128, 128), :]
                    return sums.at[n, p, rows_at(half * 512 + block * 128 + h * 64, 64), :]
                if i < RELAYED:
                    outer[half].append(Scatter(a, piece, rs1.at[n, half, i], rs2.at[n, half, i]))
                else:
                    outer[half].append(DirectScatter(a, piece, rs3.at[n, half, i - RELAYED]))
            def piece(p, half=half):
                return half_sums.at[n, half, rows_at(p * 128, 128), :]
            inner.append(DirectScatter(b, piece, land.at[n, half]))

        def finish(half, i):
            one = outer[half][i]
            block = blocks_of(half)[i]
            if i < RELAYED:
                one.arrived()
                for h in range(2):
                    half_sums[n, half, rows_at(block * 128 + h * 64, 64), :] = (
                        one.total(h).astype(BF16)
                    )
            else:
                half_sums[n, half, rows_at(block * 128, 128), :] = one.total()

        for i in range(RELAYED):
            for half in halves:
                outer[half][i].far()
            if i >= 1:
                for half in halves:
                    outer[half][i - 1].direct()
        for half in halves:
            outer[half][RELAYED - 1].direct()
        for i in range(RELAYED, 4):
            for step in (2, 1, -1):
                for half in halves:
                    outer[half][i].start(step)
        for _ in range(3):
            fill()
        for half in halves:
            outer[half][0].relay()
        for half in halves:
            outer[half][1].relay()
        for i, step in enumerate((2, 1, -1)):
            for half in halves:
                finish(half, i)
                inner[half].start(step)
        fill()
        for half in halves:
            finish(half, 3)

        inner_gather = []
        outer_gather = [[], []]

        def hand_over(half, p, block):
            ref = result.at[c * 4 + p, half * 4 + block]
            pltpu.make_async_remote_copy(
                src_ref=ref, dst_ref=ref, send_sem=across_send.at[n], recv_sem=across_recv.at[n],
                device_id=peer, device_id_type=MESH,
            ).start()

        def spread(half, block):
            a = axes[half][0]
            def place(p, h=None):
                if h is None:
                    return result.at[c * 4 + p, half * 4 + block]
                return result.at[c * 4 + p, half * 4 + block, pl.ds(h * 64, 64), :]
            if len(outer_gather[half]) < 3:
                g = Gather(a, place)
                g.start()
            else:
                g = DirectGather(a, place)
            outer_gather[half].append((g, block))
            hand_over(half, rank[a], block)

        for half, (a, b) in enumerate(axes):
            chunk = c * 4 + rank[a]
            result[chunk, half * 4 + rank[b]] = inner[half].total()
            def place(p, half=half, chunk=chunk):
                return result.at[chunk, half * 4 + p]
            inner_gather.append(DirectGather(b, place))
            spread(half, rank[b])

        def spread_relay(half, i):
            g, block = outer_gather[half][i]
            r = rank[axes[half][0]]
            if i < 3:
                g.relay_up()
            else:
                g.arrived(1)
            hand_over(half, mod4(r - 1), block)
            if i < 3:
                g.relay_down()
            else:
                g.arrived(-1)
            hand_over(half, mod4(r + 1), block)

        def spread_finish(half, i):
            g, block = outer_gather[half][i]
            if i < 3:
                g.finish()
            else:
                g.arrived(2)
            hand_over(half, mod4(rank[axes[half][0]] + 2), block)

        for _ in range(3):
            fill()
        for half in halves:
            r = rank[axes[half][1]]
            inner_gather[half].arrived(1)
            spread(half, mod4(r - 1))
            inner_gather[half].arrived(-1)
            spread(half, mod4(r + 1))
        for half in halves:
            spread_relay(half, 0)
        for half in halves:
            inner_gather[half].arrived(2)
            spread(half, mod4(rank[axes[half][1]] + 2))
        for half in halves:
            spread_relay(half, 1)
            spread_relay(half, 2)
        fill()
        for half in halves:
            spread_finish(half, 0)
        for half in halves:
            spread_relay(half, 3)
        for half in halves:
            for i in range(1, 4):
                spread_finish(half, i)
        across = pltpu.make_async_remote_copy(
            src_ref=result.at[pl.ds(c * 4, 4)], dst_ref=result.at[pl.ds((1 - c) * 4, 4)],
            send_sem=across_send.at[n], recv_sem=across_recv.at[n],
            device_id=peer, device_id_type=MESH,
        )
        across.wait_send()
        across.wait_recv()
        bytes_sent = tok.at[pl.ds(0, 960), :]
        pltpu.make_async_remote_copy(
            src_ref=bytes_sent, dst_ref=bytes_sent, send_sem=plane_send.at[n],
            recv_sem=plane_send.at[n], device_id=peer, device_id_type=MESH,
        ).wait_send()
        phase.pop()

    table_half = send(tab_send, tab6.at[pl.ds(c * 3, 3)], peer)
    table_half.wait_recv()
    for b in range(8):
        block = ids[b]
        owner = block // 3
        owner_dp = owner // 4
        here = jnp.logical_and(lax.rem(owner, 4) == z, owner_dp // 2 == x)
        slot = lax.rem(owner_dp, 2) * 3 + lax.rem(block, 3)
        for k in range(4):
            sums[0, k, b * BLOCK:(b + 1) * BLOCK, :] = jnp.where(
                here, tab6[slot, k].astype(F32), 0.0
            ).astype(BF16)
    plane_all_reduce(0, rows, lambda: None)

    tok_copy.wait()
    targets_copy.wait()

    def logits_of(start, size):
        @pl.loop(0, 4)
        def _(n):
            total = jnp.zeros((size, 256), F32)
            for k in range(8):
                total += lax.dot_general(
                    tok[rows_at(start, size), k * 256:(k + 1) * 256],
                    rows[k, pl.ds(n * 2, 2)].reshape(256, 256),
                    (((1,), (1,)), ((), ())),
                    preferred_element_type=F32,
                )
            part[rows_at(start, size), pl.ds(pl.multiple_of(n * 256, 256), 256)] = total * SCALE

    def encode(start):
        @pl.loop(0, 4)
        def _(t):
            some = rows_at(start + t * 16, 16)
            value = part[some, :]
            peak = jnp.max(jnp.abs(value), axis=1, keepdims=True)
            power = jnp.ceil(jnp.log(jnp.maximum(peak, 1e-18)) * LOG_STEP)
            steps = value * (jnp.exp(power * (-1.0 / LOG_STEP)) * STEPS)
            wire[some, :1024] = jnp.round(steps).astype(jnp.int32).astype(WIRE)
            wire[some, 1024:] = jnp.broadcast_to(power, (16, 128)).astype(jnp.int32).astype(WIRE)

    def decode(message):
        power = message[:, 1024:].astype(F32)[:, :1]
        return message[:, :1024].astype(F32) * (jnp.exp(power * (1.0 / LOG_STEP)) * (1.0 / STEPS))

    class LogitScatter(Scatter):
        def __init__(self, u):
            self.u = u
            super().__init__("y", self.encoded, y1.at[u], y2.at[u])

        def start(self, p, h):
            return pl.multiple_of(p * 256 + self.u * 128 + h * 64, 64)

        def encoded(self, p, h):
            encode(self.start(p, h))
            return wire.at[rows_at(self.start(p, h), 64), :]

        def add(self, p, h, more):
            @pl.loop(0, 4)
            def _(t):
                part[rows_at(self.start(p, h) + t * 16, 16), :] += decode(more[rows_at(t * 16, 16), :])
            return self.encoded(p, h)

    parts = [LogitScatter(u) for u in range(2)]
    for u in range(2):
        logits_of(mod4(y + 2) * 256 + u * 128, 128)
        parts[u].far()
    logits_of(mod4(y + 1) * 256, 256)
    parts[0].direct_up()
    logits_of(mod4(y - 1) * 256, 256)
    parts[0].direct_down()
    parts[0].relay()
    parts[1].direct()
    logits_of(y * 256, 256)
    parts[1].relay()

    gathers = []
    for u in range(2):
        parts[u].arrived()
        line = target[pl.ds(y * 2 + u, 1), :].astype(F32)
        column[...] = jnp.transpose(jnp.broadcast_to(line, (128, 128)))

        @pl.loop(0, 4)
        def _(t):
            h, some = t // 2, rows_at(lax.rem(t, 2) * 32, 32)
            logits = (
                part[rows_at(y * 256 + u * 128 + t * 32, 32), :]
                + decode(y2[u, 0, h, some, :])
                + decode(y2[u, 1, h, some, :])
            )
            exponent = jnp.exp(logits - jnp.max(logits, axis=1, keepdims=True))
            probability = exponent * (1.0 / jnp.sum(exponent, axis=1, keepdims=True))
            place = lax.broadcasted_iota(jnp.int32, (32, 1024), 1).astype(F32)
            onehot = jnp.where(column[rows_at(t * 32, 32), :1] == place, 1.0, 0.0)
            dl[rows_at(y * 256 + u * 128 + t * 32, 32), :] = (probability - onehot).astype(BF16)

        def dl_place(p, h, u=u):
            if h is None:
                return dl.at[rows_at(p * 256 + u * 128, 128), :]
            return dl.at[rows_at(p * 256 + u * 128 + h * 64, 64), :]

        g = Gather("y", dl_place)
        g.start()
        gathers.append(g)
    gathers[0].relay()

    def turn(p):
        dl_t[p] = jnp.transpose(dl[rows_at(p * 256, 256), :])

    def product(p, k, n):
        return jnp.dot(
            dl_t[p, rows_at(n * 512, 512), :],
            tok[rows_at(p * 256, 256), pl.ds(pl.multiple_of(k * 256, 256), 256)],
            preferred_element_type=F32,
        )

    def each_tile(f):
        @pl.loop(0, 8)
        def _(k):
            @pl.loop(0, 2)
            def _(n):
                f(k, n)

    turn(y)

    def first(k, n):
        acc[k, rows_at(n * 512, 512), :] = product(y, k, n)

    each_tile(first)
    gathers[1].relay()
    up, down, far = mod4(y + 1), mod4(y - 1), mod4(y + 2)
    turn(up)
    turn(down)

    def second(k, n):
        acc[k, rows_at(n * 512, 512), :] += product(up, k, n) + product(down, k, n)

    each_tile(second)
    for g in gathers:
        g.finish()
    turn(far)

    g_send = sums.at[0]
    crossing = []
    for q in range(4):
        k = (1 - c) * 4 + q
        @pl.loop(0, 2)
        def _(n):
            here = rows_at(n * 512, 512)
            g_send[q, here, :] = ((acc[k, here, :] + product(far, k, n)) * SCALE).astype(BF16)
        crossing.append(send(g_send.at[q], g_recv.at[q], peer))
    for q in range(4):
        k = c * 4 + q
        crossing[q].wait_recv()
        @pl.loop(0, 2)
        def _(n):
            here = rows_at(n * 512, 512)
            total = (acc[k, here, :] + product(far, k, n)) * SCALE
            sums[1, q, here, :] = (total + g_recv[q, here, :].astype(F32)).astype(BF16)
    chunks = iter(range(8))

    def token_chunk():
        k = next(chunks)

        @pl.loop(0, 2)
        def _(n):
            here = rows_at(n * 512, 512)
            tok[here, k * 256:(k + 1) * 256] = (
                jnp.dot(dl[here, :], rows[k].reshape(1024, 256), preferred_element_type=F32) * SCALE
            ).astype(BF16)

    plane_all_reduce(1, grad, token_chunk)
    assert next(chunks, None) is None
    tok_out_copy = load(tok, tok_out, 2)
    for j in range(3):
        place = 0
        for b in range(8):
            place += b * (ids[b] == (dp * 4 + z) * 3 + j).astype(jnp.int32)
        place = jnp.minimum(place, 7)
        for k in range(8):
            picked[j * BLOCK:(j + 1) * BLOCK, k * 256:(k + 1) * 256] = grad[k, place]
    grad_copy = load(picked, grad_out, 3)

    assert (len(pending), len(landed)) == (N_SEND, N_RECV), (len(pending), len(landed))
    for copy in pending:
        copy.wait_send()
    tok_out_copy.wait()
    grad_copy.wait()


def communicate(ids, tokens, table, targets):
    vmem = pltpu.VMEM
    return pl.pallas_call(
        comm_kernel,
        out_shape=(
            jax.ShapeDtypeStruct((1024, 2048), BF16),
            jax.ShapeDtypeStruct((384, 2048), BF16),
        ),
        in_specs=[
            pl.BlockSpec(memory_space=pltpu.SMEM),
            pl.BlockSpec(memory_space=pltpu.HBM),
            pl.BlockSpec(memory_space=pltpu.HBM),
            pl.BlockSpec(memory_space=pltpu.HBM),
        ],
        out_specs=(pl.BlockSpec(memory_space=pl.ANY),) * 2,
        scratch_shapes=[
            vmem((1024, 2048), BF16),
            vmem((8, 128), jnp.int32),
            vmem((6, 4, 128, 256), BF16),
            vmem((3, 4, 128, 256), BF16),
            vmem((8, 8, 128, 256), BF16),
            vmem((1024, 1024), F32),
            vmem((1024, 1152), WIRE),
            vmem((1024, 1024), BF16),
            vmem((4, 1024, 256), BF16),
            vmem((8, 1024, 256), F32),
            vmem((4, 1024, 256), BF16),
            vmem((8, 8, 128, 256), BF16),
            vmem((384, 2048), BF16),
            vmem((2, 4, 1024, 256), BF16),
            vmem((2, 2, 512, 256), BF16),
            vmem((2, 2, RELAYED, 2, 64, 256), BF16),
            vmem((2, 2, RELAYED, 2, 2, 64, 256), BF16),
            vmem((2, 2, 4 - RELAYED, 3, 128, 256), BF16),
            vmem((2, 2, 3, 128, 256), BF16),
            vmem((2, 2, 64, 1152), WIRE),
            vmem((2, 2, 2, 64, 1152), WIRE),
            vmem((128, 128), F32),
            pltpu.SemaphoreType.DMA((N_SEND,)),
            pltpu.SemaphoreType.DMA((N_RECV,)),
            pltpu.SemaphoreType.DMA((2,)),
            pltpu.SemaphoreType.DMA((13,)),
            pltpu.SemaphoreType.DMA((2,)),
            pltpu.SemaphoreType.DMA((2,)),
        ],
        compiler_params=pltpu.CompilerParams(
            collective_id=0, has_side_effects=True, vmem_limit_bytes=56 * 2**20
        ),
    )(ids, tokens, table, targets)


def update_kernel(ids, grad, w, m, v, tok_in, w_out, m_out, v_out, tok_out):
    mine = (lax.axis_index('dp') * 4 + lax.axis_index('vocab')) * 3
    size = w.shape[0] // 3
    tok_out[...] = tok_in[...]
    for part in range(3):
        here = slice(part * size, (part + 1) * size)
        block = mine + (pl.program_id(0) * 3 * size + part * size) // BLOCK
        listed = ids[0] == block
        for b in range(1, 8):
            listed = jnp.logical_or(listed, ids[b] == block)
        old = (w[here, :], m[here, :], v[here, :])
        new = adamw_rows(*old, grad[here, :].astype(F32))
        w_out[here, :] = jnp.where(listed, new[0], old[0])
        m_out[here, :] = jnp.where(listed, new[1], old[1])
        v_out[here, :] = jnp.where(listed, new[2], old[2])


def update(ids, grad, table, moment_one, moment_two, token_grads):
    wide = pl.BlockSpec((384 // STEPS_UPDATE, 2048), lambda k: (k, 0))
    tall = pl.BlockSpec((1024 // STEPS_UPDATE, 2048), lambda k: (k, 0))
    return pl.pallas_call(
        update_kernel,
        grid=(STEPS_UPDATE,),
        in_specs=[pl.BlockSpec(memory_space=pltpu.SMEM), wide, wide, wide, wide, tall],
        out_specs=[wide, wide, wide, tall],
        out_shape=[jax.ShapeDtypeStruct((384, 2048), F32)] * 3
        + [jax.ShapeDtypeStruct((1024, 2048), BF16)],
        compiler_params=pltpu.CompilerParams(vmem_limit_bytes=47 * 2**20),
    )(ids, grad, table, moment_one, moment_two, token_grads)


def body(tokens, table, moment_one, moment_two, block_ids, targets):
    token_grads, grad = communicate(block_ids, tokens, table, targets.reshape(8, 128))
    return tuple(update(block_ids, grad, table, moment_one, moment_two, token_grads))


def solution(mesh):
    wide = P(("dp", "vocab"), "width")
    return jax.shard_map(
        body,
        mesh=mesh,
        in_specs=(wide, wide, wide, wide, P(), P(("dp", "vocab"))),
        out_specs=(wide, wide, wide, wide),
        check_vma=False,
    )
```

```python
import functools
import math

import jax
import jax.numpy as jnp
from jax import lax
from jax.experimental import pallas as pl
from jax.experimental.pallas import tpu as pltpu
from jax.sharding import PartitionSpec as P

D = 8192
BLOCK = 128
SCALE = 1.0 / math.sqrt(D)
MESH = pl.DeviceIdType.MESH
BF16 = jnp.bfloat16
F32 = jnp.float32
WIRE = jnp.int16
STEPS = 32700.0
LOG_STEP = 256.0

beta_one = 0.9
beta_two = 0.95
learn_rate = 0.01
decay_rate = 0.1
epsilon = 1e-08

RELAYED = 2
STEPS_UPDATE = 2
N_SEND = 25
N_RECV = 181


def adamw_rows(weights, first, second, grads):
    first_new = beta_one * first + (1.0 - beta_one) * grads
    second_new = beta_two * second + (1.0 - beta_two) * grads * grads
    correct_one = 1.0 - beta_one**10
    correct_two = 1.0 - beta_two**10
    squared = second_new * (1.0 / correct_two)
    update = (
        first_new * (1.0 / correct_one) / (squared * lax.rsqrt(squared) + epsilon)
        + decay_rate * weights
    )
    return (weights - learn_rate * update, first_new, second_new)


def mod4(v):
    return lax.rem(v + 4, 4)


def rows_at(start, size):
    return pl.ds(pl.multiple_of(start, size), size)


def comm_kernel(
    ids, tokens, table, targets,
    tok_out, grad_out,
    tok, target, tab6, tab_send, rows, part, wire, dl, dl_t, acc, g_recv, grad, picked,
    sums, half_sums, rs1, rs2, rs3, land, y1, y2, column,
    send_sem, recv_sem, plane_send, local_sem, across_send, across_recv,
):
    dp = lax.axis_index("dp")
    z = lax.axis_index("vocab")
    y = lax.axis_index("width")
    x = dp // 2
    c = lax.rem(dp, 2)
    rank = {"x": x, "z": z, "y": y}
    pending = []

    def near(axis, step):
        if axis == "x":
            return (mod4(x + step) * 2 + c, z, y)
        if axis == "z":
            return (dp, mod4(z + step), y)
        return (dp, z, mod4(y + step))

    peer = (x * 2 + (1 - c), z, y)

    landed = []
    phase = []

    def send(src, dst, device):
        left = plane_send.at[phase[0]] if phase else send_sem.at[len(pending)]
        copy = pltpu.make_async_remote_copy(
            src_ref=src, dst_ref=dst, send_sem=left, recv_sem=recv_sem.at[len(landed)],
            device_id=device, device_id_type=MESH,
        )
        copy.start()
        landed.append(copy)
        if not phase:
            pending.append(copy)
        return copy

    def load(src, dst, i):
        copy = pltpu.make_async_copy(src, dst, local_sem.at[i])
        copy.start()
        return copy

    tab_copies = [
        load(table.at[:, k * 256:(k + 1) * 256], acc.at[k, :384, :], 5 + k) for k in range(8)
    ]
    tok_copy = load(tokens, tok, 1)
    targets_copy = load(targets, target, 0)

    barrier = pltpu.get_barrier_semaphore()
    partners = [near(a, s) for a in "xzy" for s in (1, -1)] + [near("x", 2), near("z", 2), peer]
    for device in partners:
        pl.semaphore_signal(barrier, inc=1, device_id=device, device_id_type=MESH)

    for copy in tab_copies:
        copy.wait()
    for k in range(4):
        for j in range(3):
            tab_send[j, k] = acc[(1 - c) * 4 + k, j * BLOCK:(j + 1) * BLOCK, :].astype(BF16)
    for k in range(4):
        for j in range(3):
            tab6[c * 3 + j, k] = acc[c * 4 + k, j * BLOCK:(j + 1) * BLOCK, :].astype(BF16)
    pl.semaphore_wait(barrier, len(partners))

    class Scatter:
        def __init__(self, axis, piece, first, second):
            self.axis, self.piece, self.first, self.second = axis, piece, first, second
            self.r = rank[axis]
            self.above, self.below = mod4(self.r + 1), mod4(self.r - 1)
            self.up, self.down = near(axis, 1), near(axis, -1)

        def far(self):
            far = mod4(self.r + 2)
            self.far_up = send(self.piece(far, 0), self.first.at[0], self.up)
            self.far_down = send(self.piece(far, 1), self.first.at[1], self.down)

        def direct_up(self):
            self.own_up = send(self.piece(self.above, 1), self.second.at[0, 1], self.up)

        def direct_down(self):
            self.own_down = send(self.piece(self.below, 0), self.second.at[1, 0], self.down)

        def direct(self):
            self.direct_up()
            self.direct_down()

        def add(self, p, h, more):
            ref = self.piece(p, h)
            ref[...] = (ref[...].astype(F32) + more[...].astype(F32)).astype(ref.dtype)
            return ref

        def relay_up(self):
            self.far_up.wait_recv()
            ref = self.add(self.above, 0, self.first.at[0])
            self.sum_up = send(ref, self.second.at[0, 0], self.up)

        def relay_down(self):
            self.far_down.wait_recv()
            ref = self.add(self.below, 1, self.first.at[1])
            self.sum_down = send(ref, self.second.at[1, 1], self.down)

        def relay(self):
            self.relay_up()
            self.relay_down()

        def arrived(self):
            self.sum_up.wait_recv()
            self.own_down.wait_recv()
            self.own_up.wait_recv()
            self.sum_down.wait_recv()

        def total(self, h):
            return (
                self.piece(self.r, h)[...].astype(F32)
                + self.second[0, h].astype(F32)
                + self.second[1, h].astype(F32)
            )

    class DirectScatter:
        def __init__(self, axis, piece, land):
            self.axis, self.piece, self.land = axis, piece, land
            self.r = rank[axis]
            self.sent = []

        def start(self, step):
            src = self.piece(mod4(self.r + step))
            self.sent.append(send(src, self.land.at[len(self.sent)], near(self.axis, step)))

        def total(self):
            for copy in self.sent:
                copy.wait_recv()
            value = self.piece(self.r)[...].astype(F32)
            for i in range(3):
                value += self.land[i].astype(F32)
            return value.astype(BF16)

    class DirectGather:
        def __init__(self, axis, place):
            own = place(rank[axis])
            self.sent = {step: send(own, own, near(axis, step)) for step in (1, -1, 2)}

        def arrived(self, step):
            self.sent[step].wait_recv()

    class Gather:
        def __init__(self, axis, place):
            self.axis, self.place = axis, place
            self.r = rank[axis]

        def start(self):
            own = self.place(self.r, None)
            self.up = send(own, own, near(self.axis, 1))
            self.down = send(own, own, near(self.axis, -1))

        def relay_up(self):
            self.up.wait_recv()
            ref = self.place(mod4(self.r - 1), 0)
            self.next_up = send(ref, ref, near(self.axis, 1))

        def relay_down(self):
            self.down.wait_recv()
            ref = self.place(mod4(self.r + 1), 1)
            self.next_down = send(ref, ref, near(self.axis, -1))

        def relay(self):
            self.relay_up()
            self.relay_down()

        def finish(self):
            self.next_up.wait_recv()
            self.next_down.wait_recv()

    def plane_all_reduce(n, result, fill):
        phase.append(n)
        halves = range(2)
        axes = (("x", "z"), ("z", "x"))

        def blocks_of(half):
            r = rank[axes[half][1]]
            return [mod4(r + 2), mod4(r + 1), mod4(r - 1), r]

        outer = [[], []]
        inner = []
        for half, (a, b) in enumerate(axes):
            for i, block in enumerate(blocks_of(half)):
                def piece(p, h=None, half=half, block=block):
                    if h is None:
                        return sums.at[n, p, rows_at(half * 512 + block * 128, 128), :]
                    return sums.at[n, p, rows_at(half * 512 + block * 128 + h * 64, 64), :]
                if i < RELAYED:
                    outer[half].append(Scatter(a, piece, rs1.at[n, half, i], rs2.at[n, half, i]))
                else:
                    outer[half].append(DirectScatter(a, piece, rs3.at[n, half, i - RELAYED]))
            def piece(p, half=half):
                return half_sums.at[n, half, rows_at(p * 128, 128), :]
            inner.append(DirectScatter(b, piece, land.at[n, half]))

        def finish(half, i):
            one = outer[half][i]
            block = blocks_of(half)[i]
            if i < RELAYED:
                one.arrived()
                for h in range(2):
                    half_sums[n, half, rows_at(block * 128 + h * 64, 64), :] = (
                        one.total(h).astype(BF16)
                    )
            else:
                half_sums[n, half, rows_at(block * 128, 128), :] = one.total()

        for i in range(RELAYED):
            for half in halves:
                outer[half][i].far()
            if i >= 1:
                for half in halves:
                    outer[half][i - 1].direct()
        for half in halves:
            outer[half][RELAYED - 1].direct()
        for i in range(RELAYED, 4):
            for step in (2, 1, -1):
                for half in halves:
                    outer[half][i].start(step)
        for _ in range(3):
            fill()
        for half in halves:
            outer[half][0].relay()
        for half in halves:
            outer[half][1].relay()
        for i, step in enumerate((2, 1, -1)):
            for half in halves:
                finish(half, i)
                inner[half].start(step)
        fill()
        for half in halves:
            finish(half, 3)

        inner_gather = []
        outer_gather = [[], []]

        def hand_over(half, p, block):
            ref = result.at[c * 4 + p, half * 4 + block]
            pltpu.make_async_remote_copy(
                src_ref=ref, dst_ref=ref, send_sem=across_send.at[n], recv_sem=across_recv.at[n],
                device_id=peer, device_id_type=MESH,
            ).start()

        def spread(half, block):
            a = axes[half][0]
            def place(p, h=None):
                if h is None:
                    return result.at[c * 4 + p, half * 4 + block]
                return result.at[c * 4 + p, half * 4 + block, pl.ds(h * 64, 64), :]
            if len(outer_gather[half]) < 3:
                g = Gather(a, place)
                g.start()
            else:
                g = DirectGather(a, place)
            outer_gather[half].append((g, block))
            hand_over(half, rank[a], block)

        for half, (a, b) in enumerate(axes):
            chunk = c * 4 + rank[a]
            result[chunk, half * 4 + rank[b]] = inner[half].total()
            def place(p, half=half, chunk=chunk):
                return result.at[chunk, half * 4 + p]
            inner_gather.append(DirectGather(b, place))
            spread(half, rank[b])

        def spread_relay(half, i):
            g, block = outer_gather[half][i]
            r = rank[axes[half][0]]
            if i < 3:
                g.relay_up()
            else:
                g.arrived(1)
            hand_over(half, mod4(r - 1), block)
            if i < 3:
                g.relay_down()
            else:
                g.arrived(-1)
            hand_over(half, mod4(r + 1), block)

        def spread_finish(half, i):
            g, block = outer_gather[half][i]
            if i < 3:
                g.finish()
            else:
                g.arrived(2)
            hand_over(half, mod4(rank[axes[half][0]] + 2), block)

        for _ in range(3):
            fill()
        for half in halves:
            r = rank[axes[half][1]]
            inner_gather[half].arrived(1)
            spread(half, mod4(r - 1))
            inner_gather[half].arrived(-1)
            spread(half, mod4(r + 1))
        for half in halves:
            spread_relay(half, 0)
        for half in halves:
            inner_gather[half].arrived(2)
            spread(half, mod4(rank[axes[half][1]] + 2))
        for half in halves:
            spread_relay(half, 1)
            spread_relay(half, 2)
        fill()
        for half in halves:
            spread_finish(half, 0)
        for half in halves:
            spread_relay(half, 3)
        for half in halves:
            for i in range(1, 4):
                spread_finish(half, i)
        across = pltpu.make_async_remote_copy(
            src_ref=result.at[pl.ds(c * 4, 4)], dst_ref=result.at[pl.ds((1 - c) * 4, 4)],
            send_sem=across_send.at[n], recv_sem=across_recv.at[n],
            device_id=peer, device_id_type=MESH,
        )
        across.wait_send()
        across.wait_recv()
        bytes_sent = tok.at[pl.ds(0, 960), :]
        pltpu.make_async_remote_copy(
            src_ref=bytes_sent, dst_ref=bytes_sent, send_sem=plane_send.at[n],
            recv_sem=plane_send.at[n], device_id=peer, device_id_type=MESH,
        ).wait_send()
        phase.pop()

    table_half = send(tab_send, tab6.at[pl.ds(c * 3, 3)], peer)
    table_half.wait_recv()
    for b in range(8):
        block = ids[b]
        owner = block // 3
        owner_dp = owner // 4
        here = jnp.logical_and(lax.rem(owner, 4) == z, owner_dp // 2 == x)
        slot = lax.rem(owner_dp, 2) * 3 + lax.rem(block, 3)
        for k in range(4):
            sums[0, k, b * BLOCK:(b + 1) * BLOCK, :] = jnp.where(
                here, tab6[slot, k].astype(F32), 0.0
            ).astype(BF16)
    plane_all_reduce(0, rows, lambda: None)

    tok_copy.wait()
    targets_copy.wait()

    def logits_of(start, size):
        @pl.loop(0, 4)
        def _(n):
            total = jnp.zeros((size, 256), F32)
            for k in range(8):
                total += lax.dot_general(
                    tok[rows_at(start, size), k * 256:(k + 1) * 256],
                    rows[k, pl.ds(n * 2, 2)].reshape(256, 256),
                    (((1,), (1,)), ((), ())),
                    preferred_element_type=F32,
                )
            part[rows_at(start, size), pl.ds(pl.multiple_of(n * 256, 256), 256)] = total * SCALE

    def encode(start):
        @pl.loop(0, 4)
        def _(t):
            some = rows_at(start + t * 16, 16)
            value = part[some, :]
            peak = jnp.max(jnp.abs(value), axis=1, keepdims=True)
            power = jnp.ceil(jnp.log(jnp.maximum(peak, 1e-18)) * LOG_STEP)
            steps = value * (jnp.exp(power * (-1.0 / LOG_STEP)) * STEPS)
            wire[some, :1024] = jnp.round(steps).astype(jnp.int32).astype(WIRE)
            wire[some, 1024:] = jnp.broadcast_to(power, (16, 128)).astype(jnp.int32).astype(WIRE)

    def decode(message):
        power = message[:, 1024:].astype(F32)[:, :1]
        return message[:, :1024].astype(F32) * (jnp.exp(power * (1.0 / LOG_STEP)) * (1.0 / STEPS))

    class LogitScatter(Scatter):
        def __init__(self, u):
            self.u = u
            super().__init__("y", self.encoded, y1.at[u], y2.at[u])

        def start(self, p, h):
            return pl.multiple_of(p * 256 + self.u * 128 + h * 64, 64)

        def encoded(self, p, h):
            encode(self.start(p, h))
            return wire.at[rows_at(self.start(p, h), 64), :]

        def add(self, p, h, more):
            @pl.loop(0, 4)
            def _(t):
                part[rows_at(self.start(p, h) + t * 16, 16), :] += decode(more[rows_at(t * 16, 16), :])
            return self.encoded(p, h)

    parts = [LogitScatter(u) for u in range(2)]
    for u in range(2):
        logits_of(mod4(y + 2) * 256 + u * 128, 128)
        parts[u].far()
    logits_of(mod4(y + 1) * 256, 256)
    parts[0].direct_up()
    logits_of(mod4(y - 1) * 256, 256)
    parts[0].direct_down()
    parts[0].relay()
    parts[1].direct()
    logits_of(y * 256, 256)
    parts[1].relay()

    gathers = []
    for u in range(2):
        parts[u].arrived()
        line = target[pl.ds(y * 2 + u, 1), :].astype(F32)
        column[...] = jnp.transpose(jnp.broadcast_to(line, (128, 128)))

        @pl.loop(0, 4)
        def _(t):
            h, some = t // 2, rows_at(lax.rem(t, 2) * 32, 32)
            logits = (
                part[rows_at(y * 256 + u * 128 + t * 32, 32), :]
                + decode(y2[u, 0, h, some, :])
                + decode(y2[u, 1, h, some, :])
            )
            exponent = jnp.exp(logits - jnp.max(logits, axis=1, keepdims=True))
            probability = exponent * (1.0 / jnp.sum(exponent, axis=1, keepdims=True))
            place = lax.broadcasted_iota(jnp.int32, (32, 1024), 1).astype(F32)
            onehot = jnp.where(column[rows_at(t * 32, 32), :1] == place, 1.0, 0.0)
            dl[rows_at(y * 256 + u * 128 + t * 32, 32), :] = (probability - onehot).astype(BF16)

        def dl_place(p, h, u=u):
            if h is None:
                return dl.at[rows_at(p * 256 + u * 128, 128), :]
            return dl.at[rows_at(p * 256 + u * 128 + h * 64, 64), :]

        g = Gather("y", dl_place)
        g.start()
        gathers.append(g)
    gathers[0].relay()

    def turn(p):
        dl_t[p] = jnp.transpose(dl[rows_at(p * 256, 256), :])

    def product(p, k, n):
        return jnp.dot(
            dl_t[p, rows_at(n * 512, 512), :],
            tok[rows_at(p * 256, 256), pl.ds(pl.multiple_of(k * 256, 256), 256)],
            preferred_element_type=F32,
        )

    def each_tile(f):
        @pl.loop(0, 8)
        def _(k):
            @pl.loop(0, 2)
            def _(n):
                f(k, n)

    turn(y)

    def first(k, n):
        acc[k, rows_at(n * 512, 512), :] = product(y, k, n)

    each_tile(first)
    gathers[1].relay()
    up, down, far = mod4(y + 1), mod4(y - 1), mod4(y + 2)
    turn(up)
    turn(down)

    def second(k, n):
        acc[k, rows_at(n * 512, 512), :] += product(up, k, n) + product(down, k, n)

    each_tile(second)
    for g in gathers:
        g.finish()
    turn(far)

    g_send = sums.at[0]
    crossing = []
    for q in range(4):
        k = (1 - c) * 4 + q
        @pl.loop(0, 2)
        def _(n):
            here = rows_at(n * 512, 512)
            g_send[q, here, :] = ((acc[k, here, :] + product(far, k, n)) * SCALE).astype(BF16)
        crossing.append(send(g_send.at[q], g_recv.at[q], peer))
    for q in range(4):
        k = c * 4 + q
        crossing[q].wait_recv()
        @pl.loop(0, 2)
        def _(n):
            here = rows_at(n * 512, 512)
            total = (acc[k, here, :] + product(far, k, n)) * SCALE
            sums[1, q, here, :] = (total + g_recv[q, here, :].astype(F32)).astype(BF16)
    chunks = iter(range(8))

    def token_chunk():
        k = next(chunks)

        @pl.loop(0, 2)
        def _(n):
            here = rows_at(n * 512, 512)
            tok[here, k * 256:(k + 1) * 256] = (
                jnp.dot(dl[here, :], rows[k].reshape(1024, 256), preferred_element_type=F32) * SCALE
            ).astype(BF16)

    plane_all_reduce(1, grad, token_chunk)
    assert next(chunks, None) is None
    tok_out_copy = load(tok, tok_out, 2)
    for j in range(3):
        place = 0
        for b in range(8):
            place += b * (ids[b] == (dp * 4 + z) * 3 + j).astype(jnp.int32)
        place = jnp.minimum(place, 7)
        for k in range(8):
            picked[j * BLOCK:(j + 1) * BLOCK, k * 256:(k + 1) * 256] = grad[k, place]
    grad_copy = load(picked, grad_out, 3)

    assert (len(pending), len(landed)) == (N_SEND, N_RECV), (len(pending), len(landed))
    for copy in pending:
        copy.wait_send()
    tok_out_copy.wait()
    grad_copy.wait()


def communicate(ids, tokens, table, targets):
    vmem = pltpu.VMEM
    return pl.pallas_call(
        comm_kernel,
        out_shape=(
            jax.ShapeDtypeStruct((1024, 2048), BF16),
            jax.ShapeDtypeStruct((384, 2048), BF16),
        ),
        in_specs=[
            pl.BlockSpec(memory_space=pltpu.SMEM),
            pl.BlockSpec(memory_space=pltpu.HBM),
            pl.BlockSpec(memory_space=pltpu.HBM),
            pl.BlockSpec(memory_space=pltpu.HBM),
        ],
        out_specs=(pl.BlockSpec(memory_space=pl.ANY),) * 2,
        scratch_shapes=[
            vmem((1024, 2048), BF16),
            vmem((8, 128), jnp.int32),
            vmem((6, 4, 128, 256), BF16),
            vmem((3, 4, 128, 256), BF16),
            vmem((8, 8, 128, 256), BF16),
            vmem((1024, 1024), F32),
            vmem((1024, 1152), WIRE),
            vmem((1024, 1024), BF16),
            vmem((4, 1024, 256), BF16),
            vmem((8, 1024, 256), F32),
            vmem((4, 1024, 256), BF16),
            vmem((8, 8, 128, 256), BF16),
            vmem((384, 2048), BF16),
            vmem((2, 4, 1024, 256), BF16),
            vmem((2, 2, 512, 256), BF16),
            vmem((2, 2, RELAYED, 2, 64, 256), BF16),
            vmem((2, 2, RELAYED, 2, 2, 64, 256), BF16),
            vmem((2, 2, 4 - RELAYED, 3, 128, 256), BF16),
            vmem((2, 2, 3, 128, 256), BF16),
            vmem((2, 2, 64, 1152), WIRE),
            vmem((2, 2, 2, 64, 1152), WIRE),
            vmem((128, 128), F32),
            pltpu.SemaphoreType.DMA((N_SEND,)),
            pltpu.SemaphoreType.DMA((N_RECV,)),
            pltpu.SemaphoreType.DMA((2,)),
            pltpu.SemaphoreType.DMA((13,)),
            pltpu.SemaphoreType.DMA((2,)),
            pltpu.SemaphoreType.DMA((2,)),
        ],
        compiler_params=pltpu.CompilerParams(
            collective_id=0, has_side_effects=True, vmem_limit_bytes=56 * 2**20
        ),
    )(ids, tokens, table, targets)


def update_kernel(ids, grad, w, m, v, tok_in, w_out, m_out, v_out, tok_out):
    mine = (lax.axis_index('dp') * 4 + lax.axis_index('vocab')) * 3
    size = w.shape[0] // 3
    tok_out[...] = tok_in[...]
    for part in range(3):
        here = slice(part * size, (part + 1) * size)
        block = mine + (pl.program_id(0) * 3 * size + part * size) // BLOCK
        listed = ids[0] == block
        for b in range(1, 8):
            listed = jnp.logical_or(listed, ids[b] == block)
        old = (w[here, :], m[here, :], v[here, :])
        new = adamw_rows(*old, grad[here, :].astype(F32))
        w_out[here, :] = jnp.where(listed, new[0], old[0])
        m_out[here, :] = jnp.where(listed, new[1], old[1])
        v_out[here, :] = jnp.where(listed, new[2], old[2])


def update(ids, grad, table, moment_one, moment_two, token_grads):
    wide = pl.BlockSpec((384 // STEPS_UPDATE, 2048), lambda k: (k, 0))
    tall = pl.BlockSpec((1024 // STEPS_UPDATE, 2048), lambda k: (k, 0))
    return pl.pallas_call(
        update_kernel,
        grid=(STEPS_UPDATE,),
        in_specs=[pl.BlockSpec(memory_space=pltpu.SMEM), wide, wide, wide, wide, tall],
        out_specs=[wide, wide, wide, tall],
        out_shape=[jax.ShapeDtypeStruct((384, 2048), F32)] * 3
        + [jax.ShapeDtypeStruct((1024, 2048), BF16)],
        compiler_params=pltpu.CompilerParams(vmem_limit_bytes=47 * 2**20),
    )(ids, grad, table, moment_one, moment_two, token_grads)


def body(tokens, table, moment_one, moment_two, block_ids, targets):
    token_grads, grad = communicate(block_ids, tokens, table, targets.reshape(8, 128))
    return tuple(update(block_ids, grad, table, moment_one, moment_two, token_grads))


def solution(mesh):
    wide = P(("dp", "vocab"), "width")
    return jax.shard_map(
        body,
        mesh=mesh,
        in_specs=(wide, wide, wide, wide, P(), P(("dp", "vocab"))),
        out_specs=(wide, wide, wide, wide),
        check_vma=False,
    )
```
